512 devices in a mesh: loop: 32 (over z, x_hi), group: 16 (over x_lo, y, core).
Axes of the slice: x: 4 (x_hi: 2, x_lo: 2; x = x_hi * 2 + x_lo), y: 4, z: 16, core: 2. Of those that a mesh axis runs over, the one named last changes fastest.
Arguments:
- images: bfloat16 [262144, 1152], P(('loop', 'group')), may hold values from -24 to 24
- texts: bfloat16 [262144, 1152], P(('loop', 'group')), may hold values from -24 to 24
- log_temp: float32 [1], replicated, may hold values from 1.8 to 2.5
- logit_bias: float32 [1], replicated, may hold values from -4 to -1
Outputs:
- image_grad: bfloat16 [262144, 1152], P(('loop', 'group'))
- text_grad: bfloat16 [262144, 1152], P(('loop', 'group'))
- summary: float32 [3], replicated
The draws below stay inside these ranges and needn't reach their ends.
All inputs are finite; a program needn't handle non-finite values.
Results may differ from the reference program's by a relative error of at most 0.0034.
Values may be sent and summed in bfloat16 or wider, within the bound.
A program may use at most 64 MiB of HBM per device.

```python
import jax
import jax.numpy as jnp
from jax import lax

D = 1152
ROWS = 512
STEPS = 2
TOKENS = 262144
PAIRS = 402653184
N_LOOP = 32
N_GROUP = 16


def shaped(values):
    return values


def shared(key):
    subkeys = jax.random.split(key, 4)
    blocks = TOKENS // ROWS
    img_noise = shaped(jnp.clip(jax.random.normal(subkeys[0], (blocks, ROWS, D), jnp.float32), -8.0, 8.0))
    topics = shaped(jnp.clip(jax.random.normal(subkeys[1], (blocks, 1, D), jnp.float32), -8.0, 8.0))
    member_level = jax.random.uniform(subkeys[2], (N_GROUP,), jnp.float32, 0.0, 1.0)
    jitter = jax.random.uniform(subkeys[3], (blocks,), jnp.float32, 0.6, 1.4)
    member = jnp.arange(blocks, dtype=jnp.int32) % N_GROUP
    topic_power = 8.0 * jnp.take(member_level, member) ** 2 * jitter
    topic_term = jnp.sqrt(topic_power)[:, None, None] * topics
    row_size = (0.02 * (1.0 + 40.0 * topic_power / (1.0 + topic_power)))[:, None, None]
    return (img_noise, topic_term, row_size)


def draw_images(key, part):
    own_key = jax.random.fold_in(key, 1)
    wobble = 0.0
    img_noise, topic_term, row_size = shared(key)
    scales = jnp.exp(jax.random.uniform(own_key, (TOKENS // ROWS, ROWS, 1), jnp.float32, -wobble, wobble))
    values = (img_noise + topic_term) * row_size * scales
    return jnp.clip(values, -24.0, 24.0).reshape(TOKENS, D).astype(jnp.bfloat16)


def draw_texts(key, part):
    own_key = jax.random.fold_in(key, 2)
    wobble = 0.0
    img_noise, topic_term, row_size = shared(key)
    subkeys = jax.random.split(own_key, 3)
    blocks = TOKENS // ROWS
    txt_noise = shaped(jnp.clip(jax.random.normal(subkeys[0], (blocks, ROWS, D), jnp.float32), -8.0, 8.0))
    matched = jax.random.uniform(subkeys[1], (blocks, ROWS, 1), jnp.float32, 1.0, 2.0)
    scales = jnp.exp(jax.random.uniform(subkeys[2], (blocks, ROWS, 1), jnp.float32, -wobble, wobble))
    values = (matched * img_noise + txt_noise + topic_term) * row_size * scales
    return jnp.clip(values, -24.0, 24.0).reshape(TOKENS, D).astype(jnp.bfloat16)


def setup_inputs(seed: int = 0) -> dict:
    key_of = jax.random.split(jax.random.key(seed), 5)
    images = draw_images(jax.random.fold_in(key_of[4], 71), 0)
    texts = draw_texts(jax.random.fold_in(key_of[4], 71), 0)
    log_temp = jnp.clip(jax.random.uniform(key_of[2], (1,), jnp.float32, 1.8, 2.5), 1.8, 2.5)
    logit_bias = jnp.clip(jax.random.uniform(key_of[3], (1,), jnp.float32, -4.0, -1.0), -4.0, -1.0)
    return dict(images=images, texts=texts, log_temp=log_temp, logit_bias=logit_bias)


EPS = 1e-06

def normalize(block):
    values = block.astype(jnp.float32)
    length = jnp.sqrt(lax.optimization_barrier(jnp.sum(values * values, axis=1, keepdims=True)) + EPS)
    return (values / length, length)

def pair_terms(left, right, temper, offset, matched):
    scores = lax.dot_general(left, right, (((1,), (1,)), ((), ())), preferred_element_type=jnp.float32)
    logit = temper * scores + offset
    if matched:
        sign = jnp.where(jnp.eye(left.shape[0], dtype=bool), 1.0, -1.0).astype(jnp.float32)
    else:
        sign = -jnp.ones_like(scores)
    pair_loss = jax.nn.softplus(-sign * logit)
    slope = -sign * jax.nn.sigmoid(-sign * logit)
    weighted = (temper * slope).astype(jnp.bfloat16)
    return (pair_loss, slope, scores, weighted)

def project(unit, length, direction):
    inner = lax.optimization_barrier(jnp.sum(unit * direction, axis=1, keepdims=True))
    return ((direction - unit * inner) / length).astype(jnp.bfloat16)

def reference(images, texts, log_temp, logit_bias):
    temper = jnp.exp(log_temp[0])
    offset = logit_bias[0]
    img_blocks = images.reshape(N_LOOP, N_GROUP, ROWS, D)
    txt_blocks = texts.reshape(N_LOOP, N_GROUP, ROWS, D)
    count = N_LOOP * N_GROUP

    def image_side(index):
        position = index // N_GROUP
        member = index % N_GROUP
        unit_img, img_length = normalize(img_blocks[position, member])
        img_b = unit_img.astype(jnp.bfloat16)
        img_dir = jnp.zeros((ROWS, D), jnp.float32)
        totals = jnp.zeros((3,), jnp.float32)
        for step in range(STEPS + 1):
            source = ((position - step) % N_LOOP).astype(jnp.int32)
            unit_txt, _ = normalize(txt_blocks[source, member])
            txt_b = unit_txt.astype(jnp.bfloat16)
            pair_loss, slope, scores, weighted = pair_terms(img_b, txt_b, temper, offset, step == 0)
            img_dir = img_dir + jnp.dot(weighted, txt_b, preferred_element_type=jnp.float32)
            totals = totals + jnp.stack([jnp.sum(pair_loss), jnp.sum(slope * temper * scores), jnp.sum(slope)])
        return (project(unit_img, img_length, img_dir), totals)

    def text_side(index):
        position = index // N_GROUP
        member = index % N_GROUP
        unit_txt, txt_length = normalize(txt_blocks[position, member])
        txt_b = unit_txt.astype(jnp.bfloat16)
        txt_dir = jnp.zeros((ROWS, D), jnp.float32)
        for step in range(STEPS + 1):
            source = ((position + step) % N_LOOP).astype(jnp.int32)
            unit_img, _ = normalize(img_blocks[source, member])
            img_b = unit_img.astype(jnp.bfloat16)
            _, _, _, weighted = pair_terms(img_b, txt_b, temper, offset, step == 0)
            txt_dir = txt_dir + lax.dot_general(weighted, img_b, (((0,), (0,)), ((), ())), preferred_element_type=jnp.float32)
        return project(unit_txt, txt_length, txt_dir)
    indices = jnp.arange(count, dtype=jnp.int32)
    image_grad, totals = lax.map(image_side, indices)
    text_grad = lax.map(text_side, indices)
    summary = lax.optimization_barrier(jnp.sum(totals, axis=0)) / PAIRS
    return (image_grad.reshape(TOKENS, D), text_grad.reshape(TOKENS, D), summary)
```

```python
import functools

import jax
import jax.numpy as jnp
from jax import lax
from jax.experimental import pallas as pl
from jax.experimental.pallas import tpu as pltpu
from jax.sharding import PartitionSpec as P

STEPS = 2
EPS = 1e-06
MESH = pl.DeviceIdType.MESH

CHUNK = 64
PIECE = 128
TILE = 256
LEAD = 4

IMG, TXT, IMG2, TXT2, IMG1, TXT1 = range(6)
N_Y, N_CORE = 4, 2


def kernel(
    n_loop,
    log_temp,
    logit_bias,
    images,
    texts,
    image_grad,
    text_grad,
    summary,
    raw,
    land,
    acc,
    inverse,
    sums,
    pair_in,
    tiles_z,
    tiles_g,
    tiles_x,
    result,
    load_sem,
    store_sem,
    near_send,
    far_send,
    arrived,
    z_ready,
    pair_sem,
    z_send,
    z_recv,
    g_send,
    g_recv,
    x_send,
    x_recv,
    result_sem,
):
    rows = raw.shape[1]
    chunks = rows // CHUNK
    pieces = rows // PIECE
    per_piece = PIECE // CHUNK
    n_z = n_loop // 2

    p = lax.axis_index("loop")
    h = lax.axis_index("group")
    z, xh = p // 2, lax.rem(p, 2)
    xl, yc = h // (N_Y * N_CORE), lax.rem(h, N_Y * N_CORE)
    odd = lax.rem(z, 2) == 1
    even = lax.rem(z, 2) == 0

    def at(z_, xh_, xl_, yc_):
        return (z_ * 2 + xh_, xl_ * (N_Y * N_CORE) + yc_)

    up = lax.rem(z + 1, n_z)
    down = lax.rem(z + n_z - 1, n_z)
    across = at(z, 1 - xh, xl, yc)
    above = at(up, xh, xl, yc)
    below = at(down, xh, xl, yc)

    half = n_z // 2
    zi = z // 2
    xi = xh * 2 + xl

    def z_peer(i):
        return at(2 * i + 1, xh, xl, yc)

    def g_peer(i):
        return at(z, xh, xl, i)

    def x_peer(i):
        return at(z, i // 2, lax.rem(i, 2), yc)

    exchanges = (
        (tiles_z, zi, half, z_peer, z_send, z_recv),
        (tiles_g, yc, N_Y * N_CORE, g_peer, g_send, g_recv),
        (tiles_x, xi, 4, x_peer, x_send, x_recv),
    )

    barrier = pltpu.get_barrier_semaphore()
    pl.semaphore_signal(barrier, inc=1, device_id=across, device_id_type=MESH)

    @pl.when(even)
    def _():
        pl.semaphore_signal(barrier, inc=1, device_id=above, device_id_type=MESH)
        pl.semaphore_signal(barrier, inc=1, device_id=below, device_id_type=MESH)

    @pl.when(odd)
    def _():
        for _, index, size, peer, _, _ in exchanges:
            for k in range(1, size):
                pl.semaphore_signal(
                    barrier, inc=1, device_id=peer(lax.rem(index + k, size)), device_id_type=MESH
                )

    first = 1 - xh
    second = xh

    for block, source in ((IMG, images), (TXT, texts)):
        pltpu.make_async_copy(source, raw.at[block], load_sem.at[block]).start()
    for block, source in ((IMG, images), (TXT, texts)):
        pltpu.make_async_copy(source, raw.at[block], load_sem.at[block]).wait()

    def part(c):
        return pl.ds(pl.multiple_of(c * CHUNK, CHUNK), CHUNK)

    def normalize(block):
        def step(c, carry):
            values = raw[block, part(c)].astype(jnp.float32)
            length = jnp.sqrt(jnp.sum(values * values, axis=1, keepdims=True) + EPS)
            scale = 1.0 / length
            inverse[block, part(c)] = scale
            land[block, part(c)] = (values * scale).astype(jnp.bfloat16)
            return carry

        lax.fori_loop(0, chunks, step, 0)

    def own_copy(c):
        return pltpu.make_async_remote_copy(
            src_ref=land.at[first, part(c)],
            dst_ref=land.at[4 + first, part(c)],
            send_sem=far_send.at[0, c],
            recv_sem=arrived.at[2 + first, c],
            device_id=across,
            device_id_type=MESH,
        )

    def forward_copy(c):
        return pltpu.make_async_remote_copy(
            src_ref=land.at[2 + xh, part(c)],
            dst_ref=land.at[4 + xh, part(c)],
            send_sem=far_send.at[1, c],
            recv_sem=arrived.at[2 + xh, c],
            device_id=across,
            device_id_type=MESH,
        )

    def near_copy(block, c):
        return pltpu.make_async_remote_copy(
            src_ref=land.at[block, part(c)],
            dst_ref=land.at[2 + block, part(c)],
            send_sem=near_send.at[block, c],
            recv_sem=arrived.at[block, c],
            device_id=below if block == IMG else above,
            device_id_type=MESH,
        )

    def wait_arrival(slot, c):
        pltpu.make_async_remote_copy(
            src_ref=land.at[slot, part(c)],
            dst_ref=land.at[slot, part(c)],
            send_sem=near_send.at[0, 0],
            recv_sem=arrived.at[slot - 2, c],
            device_id=across,
            device_id_type=MESH,
        ).wait_recv()

    def loop(start, stop, body):
        def step(i, carry):
            body(i)
            return carry

        lax.fori_loop(start, stop, step, 0)

    normalize(first)

    @pl.when(even)
    def _():
        pl.semaphore_wait(barrier, 1)

    @pl.when(odd)
    def _():
        pl.semaphore_wait(barrier, 3 + sum(e[2] - 1 for e in exchanges))
        pl.semaphore_signal(z_ready, inc=1, device_id=above, device_id_type=MESH)
        pl.semaphore_signal(z_ready, inc=1, device_id=below, device_id_type=MESH)

    lead = LEAD + xh * (chunks - LEAD)
    loop(0, lead, lambda c: own_copy(c).start())
    normalize(second)

    @pl.when(even)
    def _():
        pl.semaphore_wait(z_ready, 2)

    def send_near(c):
        near_copy(IMG, c).start()
        near_copy(TXT, c).start()

    loop(0, chunks, send_near)

    temper = jnp.exp(jnp.full((1, 1), log_temp[0], jnp.float32))
    offset = logit_bias[0]
    sums[...] = jnp.zeros_like(sums)

    def fold(values):
        return jnp.sum(values.reshape(TILE // 8, 8, PIECE), axis=0)

    def piece(own, slot, i, matched, loss):
        partner = land[slot, pl.ds(pl.multiple_of(i * PIECE, PIECE), PIECE)]

        def step(t, carry):
            here = pl.ds(pl.multiple_of(t * TILE, TILE), TILE)
            scores = lax.dot_general(
                land[own, here], partner, (((1,), (1,)), ((), ())), preferred_element_type=jnp.float32
            )
            logit = temper * scores + offset
            if matched:
                shape = (TILE, PIECE)
                r = lax.broadcasted_iota(jnp.int32, shape, 0) + t * TILE
                c = lax.broadcasted_iota(jnp.int32, shape, 1) + i * PIECE
                logit = jnp.where(r == c, -logit, logit)
            small = jnp.exp(-jnp.abs(logit))
            recip = 1.0 / (1.0 + small)
            slope = jnp.where(logit >= 0, recip, small * recip)
            if matched:
                slope = jnp.where(r == c, -slope, slope)
            if loss:
                pair_loss = jnp.maximum(logit, 0.0) + jnp.log1p(small)
                sums[0] += fold(pair_loss)
                sums[1] += fold(slope * scores)
                sums[2] += fold(slope)
            weighted = (temper * slope).astype(jnp.bfloat16)
            direction = jnp.dot(weighted, partner, preferred_element_type=jnp.float32)
            if matched:

                @pl.when(i == 0)
                def _():
                    acc[own, here] = direction

                @pl.when(i > 0)
                def _():
                    acc[own, here] += direction
            else:
                acc[own, here] += direction
            return carry

        lax.fori_loop(0, rows // TILE, step, 0)

    def project(block, target):
        def step(c):
            scale = inverse[block, part(c)]
            unit = raw[block, part(c)].astype(jnp.float32) * scale
            direction = acc[block, part(c)]
            inner = jnp.sum(unit * direction, axis=1, keepdims=True)
            raw[block, part(c)] = ((direction - unit * inner) * scale).astype(jnp.bfloat16)
            pltpu.make_async_copy(raw.at[block, part(c)], target.at[part(c)], store_sem.at[block, c]).start()

        loop(0, chunks, step)

    def hand_on(c):
        wait_arrival(IMG2, c)
        wait_arrival(TXT2, c)
        forward_copy(c).start()

    def own_pieces(i):
        piece(TXT, IMG, i, True, True)
        piece(IMG, TXT, i, True, False)
        hand_on(i)

    loop(0, pieces, own_pieces)

    def near_pieces(i):
        hand_on(pieces + i)

        @pl.when(i == pieces - 1)
        def _():
            loop(lead, chunks, lambda c: own_copy(c).start())

        piece(TXT, IMG2, i, False, True)
        piece(IMG, TXT2, i, False, False)

    loop(0, pieces, near_pieces)

    def far_images(i):
        for k in range(per_piece):
            wait_arrival(IMG1, i * per_piece + k)
        piece(TXT, IMG1, i, False, True)

    loop(0, pieces, far_images)

    rows_of = lax.broadcasted_iota(jnp.int32, (8, 128), 0)
    mine = jnp.zeros((8, 128), jnp.float32)
    for k in range(3):
        total = jnp.sum(sums[k], axis=0, keepdims=True)
        mine = jnp.where(rows_of == k, jnp.broadcast_to(total, (8, 128)), mine)
    result[...] = mine

    def pair_copy(target, device):
        return pltpu.make_async_remote_copy(
            src_ref=result,
            dst_ref=target,
            send_sem=pair_sem.at[0],
            recv_sem=pair_sem.at[1],
            device_id=device,
            device_id_type=MESH,
        )

    @pl.when(even)
    def _():
        pair_copy(pair_in, above).start()

    @pl.when(odd)
    def _():
        pair_copy(pair_in, below).wait_recv()
        value = result[...] + pair_in[...]
        for tiles, index, size, peer, send, recv in exchanges:
            tiles[index] = value

            def to(k, tiles=tiles, index=index, size=size, peer=peer, send=send, recv=recv):
                return pltpu.make_async_remote_copy(
                    src_ref=tiles.at[index],
                    dst_ref=tiles.at[index],
                    send_sem=send.at[k],
                    recv_sem=recv.at[index],
                    device_id=peer(lax.rem(index + k, size)),
                    device_id_type=MESH,
                )

            for k in range(1, size):
                to(k).start()
            for k in range(1, size):
                source = lax.rem(index + k, size)
                pltpu.make_async_remote_copy(
                    src_ref=tiles.at[source],
                    dst_ref=tiles.at[source],
                    send_sem=send.at[k],
                    recv_sem=recv.at[source],
                    device_id=peer(source),
                    device_id_type=MESH,
                ).wait_recv()
            value = tiles[0]
            for k in range(1, size):
                value = value + tiles[k]
            for k in range(1, size):
                to(k).wait_send()
        result[...] = value
        pltpu.make_async_remote_copy(
            src_ref=result,
            dst_ref=pair_in,
            send_sem=result_sem.at[0],
            recv_sem=result_sem.at[1],
            device_id=below,
            device_id_type=MESH,
        ).start()

    project(TXT, text_grad)

    def far_texts(i):
        for k in range(per_piece):
            wait_arrival(TXT1, i * per_piece + k)
        piece(IMG, TXT1, i, False, False)

    loop(0, pieces, far_texts)
    project(IMG, image_grad)

    back = pltpu.make_async_remote_copy(
        src_ref=result,
        dst_ref=pair_in,
        send_sem=result_sem.at[0],
        recv_sem=result_sem.at[1],
        device_id=below,
        device_id_type=MESH,
    )

    @pl.when(even)
    def _():
        pair_copy(pair_in, above).wait_send()
        back.wait_recv()
        result[...] = pair_in[...]

    @pl.when(odd)
    def _():
        back.wait_send()

    total = jnp.sum(result[...], axis=1, keepdims=True)
    n_pairs = n_loop * lax.axis_size("group") * rows * rows * (STEPS + 1)
    total = jnp.where(lax.broadcasted_iota(jnp.int32, (8, 1), 0) == 1, temper * total, total) / n_pairs
    summary[...] = jnp.broadcast_to(total, (8, 128))

    def finish(c):
        own_copy(c).wait_send()
        forward_copy(c).wait_send()
        near_copy(IMG, c).wait_send()
        near_copy(TXT, c).wait_send()
        for block, target in ((IMG, image_grad), (TXT, text_grad)):
            pltpu.make_async_copy(raw.at[block, part(c)], target.at[part(c)], store_sem.at[block, c]).wait()

    loop(0, chunks, finish)


def body(images, texts, log_temp, logit_bias):
    rows, width = images.shape
    chunks = rows // CHUNK
    n_loop = lax.axis_size("loop")
    half = n_loop // 4
    bf16, f32, dma = jnp.bfloat16, jnp.float32, pltpu.SemaphoreType.DMA
    smem = pl.BlockSpec(memory_space=pltpu.SMEM)
    whole = pl.BlockSpec(memory_space=pl.ANY)
    image_grad, text_grad, summary = pl.pallas_call(
        functools.partial(kernel, n_loop),
        out_shape=(
            jax.ShapeDtypeStruct((rows, width), bf16),
            jax.ShapeDtypeStruct((rows, width), bf16),
            jax.ShapeDtypeStruct((8, 128), f32),
        ),
        in_specs=[smem, smem, whole, whole],
        out_specs=(whole, whole, pl.BlockSpec(memory_space=pltpu.VMEM)),
        scratch_shapes=[
            pltpu.VMEM((2, rows, width), bf16),
            pltpu.VMEM((6, rows, width), bf16),
            pltpu.VMEM((2, rows, width), f32),
            pltpu.VMEM((2, rows, 1), f32),
            pltpu.VMEM((3, 8, 128), f32),
            pltpu.VMEM((8, 128), f32),
            pltpu.VMEM((half, 8, 128), f32),
            pltpu.VMEM((N_Y * N_CORE, 8, 128), f32),
            pltpu.VMEM((4, 8, 128), f32),
            pltpu.VMEM((8, 128), f32),
            dma((2,)),
            dma((2, chunks)),
            dma((2, chunks)),
            dma((2, chunks)),
            dma((4, chunks)),
            pltpu.SemaphoreType.REGULAR,
            dma((2,)),
            dma((half,)),
            dma((half,)),
            dma((N_Y * N_CORE,)),
            dma((N_Y * N_CORE,)),
            dma((4,)),
            dma((4,)),
            dma((2,)),
        ],
        compiler_params=pltpu.CompilerParams(
            collective_id=0, has_side_effects=True, vmem_limit_bytes=40 * 2**20
        ),
        cost_estimate=pl.CostEstimate(
            flops=24 * rows * rows * width, bytes_accessed=8 * rows * width, transcendentals=2 * 6 * rows * rows
        ),
        name="exchange",
    )(log_temp, logit_bias, images, texts)
    return image_grad, text_grad, summary[:3, 0]


def solution(mesh):
    in_specs = (P(("loop", "group"), None), P(("loop", "group"), None), P(), P())
    out_specs = (P(("loop", "group"), None), P(("loop", "group"), None), P())
    return jax.shard_map(body, mesh=mesh, in_specs=in_specs, out_specs=out_specs, check_vma=False)
```

```python
import functools

import jax
import jax.numpy as jnp
from jax import lax
from jax.experimental import pallas as pl
from jax.experimental.pallas import tpu as pltpu
from jax.sharding import PartitionSpec as P

STEPS = 2
EPS = 1e-06
MESH = pl.DeviceIdType.MESH

CHUNK = 64
LAST = (256, 128, 128)
LEAD = 2
LEAD_FIRST = 5
PASS = 256

IMG, TXT, IMG2, TXT2, IMG1, TXT1 = range(6)
N_Y, N_CORE = 4, 2


def project(values, scale, direction):
    unit = values.astype(jnp.float32) * scale
    inner = jnp.sum(unit * direction, axis=1, keepdims=True)
    return ((direction - unit * inner) * scale).astype(jnp.bfloat16)


def kernel(
    n_loop,
    log_temp,
    logit_bias,
    images,
    texts,
    raw,
    acc,
    inverse,
    result,
    land,
    scalars,
    sums,
    pair_in,
    tiles_z,
    tiles_g,
    tiles_x,
    load_sem,
    near_send,
    far_send,
    arrived,
    z_ready,
    pair_sem,
    z_send,
    z_recv,
    g_send,
    g_recv,
    x_send,
    x_recv,
    result_sem,
):
    rows = raw.shape[1]
    chunks = rows // CHUNK
    n_z = n_loop // 2

    p = lax.axis_index("loop")
    h = lax.axis_index("group")
    z, xh = p // 2, lax.rem(p, 2)
    xl, yc = h // (N_Y * N_CORE), lax.rem(h, N_Y * N_CORE)
    odd = lax.rem(z, 2) == 1
    even = lax.rem(z, 2) == 0

    def at(z_, xh_, xl_, yc_):
        return (z_ * 2 + xh_, xl_ * (N_Y * N_CORE) + yc_)

    up = lax.rem(z + 1, n_z)
    down = lax.rem(z + n_z - 1, n_z)
    across = at(z, 1 - xh, xl, yc)
    above = at(up, xh, xl, yc)
    below = at(down, xh, xl, yc)

    half = n_z // 2
    zi = z // 2
    xi = xh * 2 + xl

    def z_peer(i):
        return at(2 * i + 1, xh, xl, yc)

    def g_peer(i):
        return at(z, xh, xl, i)

    def x_peer(i):
        return at(z, i // 2, lax.rem(i, 2), yc)

    exchanges = (
        (tiles_z, zi, half, z_peer, z_send, z_recv),
        (tiles_g, yc, N_Y * N_CORE, g_peer, g_send, g_recv),
        (tiles_x, xi, 4, x_peer, x_send, x_recv),
    )

    barrier = pltpu.get_barrier_semaphore()
    pl.semaphore_signal(barrier, inc=1, device_id=across, device_id_type=MESH)

    @pl.when(even)
    def _():
        pl.semaphore_signal(barrier, inc=1, device_id=above, device_id_type=MESH)
        pl.semaphore_signal(barrier, inc=1, device_id=below, device_id_type=MESH)

    @pl.when(odd)
    def _():
        for _, index, size, peer, _, _ in exchanges:
            for k in range(1, size):
                pl.semaphore_signal(
                    barrier, inc=1, device_id=peer(lax.rem(index + k, size)), device_id_type=MESH
                )

    first = 1 - xh
    second = xh

    loads = (
        (images, raw.at[IMG]),
        (texts, raw.at[TXT]),
        (log_temp, scalars.at[0]),
        (logit_bias, scalars.at[1]),
    )
    for k, (source, target) in enumerate(loads):
        pltpu.make_async_copy(source, target, load_sem.at[k]).start()
    for k, (source, target) in enumerate(loads):
        pltpu.make_async_copy(source, target, load_sem.at[k]).wait()

    def loop(start, stop, body):
        def step(i, carry):
            body(i)
            return carry

        lax.fori_loop(start, stop, step, 0)

    def part(c):
        return pl.ds(pl.multiple_of(c * CHUNK, CHUNK), CHUNK)

    def normalize(block):
        def step(c):
            here = pl.ds(pl.multiple_of(c * PASS, PASS), PASS)
            values = raw[block, here].astype(jnp.float32)
            length = jnp.sqrt(jnp.sum(values * values, axis=1, keepdims=True) + EPS)
            scale = 1.0 / length
            inverse[block, here] = scale
            land[block, here] = (values * scale).astype(jnp.bfloat16)

        loop(0, rows // PASS, step)

    def own_copy(c):
        return pltpu.make_async_remote_copy(
            src_ref=land.at[first, part(c)],
            dst_ref=land.at[4 + first, part(c)],
            send_sem=far_send.at[0, c],
            recv_sem=arrived.at[2 + first, c],
            device_id=across,
            device_id_type=MESH,
        )

    def forward_copy(c):
        return pltpu.make_async_remote_copy(
            src_ref=land.at[2 + xh, part(c)],
            dst_ref=land.at[4 + xh, part(c)],
            send_sem=far_send.at[1, c],
            recv_sem=arrived.at[2 + xh, c],
            device_id=across,
            device_id_type=MESH,
        )

    def near_copy(block, c):
        return pltpu.make_async_remote_copy(
            src_ref=land.at[block, part(c)],
            dst_ref=land.at[2 + block, part(c)],
            send_sem=near_send.at[block, c],
            recv_sem=arrived.at[block, c],
            device_id=below if block == IMG else above,
            device_id_type=MESH,
        )

    def wait_arrival(slot, c):
        pltpu.make_async_remote_copy(
            src_ref=land.at[slot, part(c)],
            dst_ref=land.at[slot, part(c)],
            send_sem=near_send.at[0, 0],
            recv_sem=arrived.at[slot - 2, c],
            device_id=across,
            device_id_type=MESH,
        ).wait_recv()

    normalize(first)

    @pl.when(even)
    def _():
        pl.semaphore_wait(barrier, 1)

    @pl.when(odd)
    def _():
        pl.semaphore_wait(barrier, 3 + sum(e[2] - 1 for e in exchanges))
        pl.semaphore_signal(z_ready, inc=1, device_id=above, device_id_type=MESH)
        pl.semaphore_signal(z_ready, inc=1, device_id=below, device_id_type=MESH)

    lead = jnp.where(xh == 1, chunks, jnp.where(z == 0, LEAD_FIRST, LEAD))
    loop(0, lead, lambda c: own_copy(c).start())
    normalize(second)

    @pl.when(even)
    def _():
        pl.semaphore_wait(z_ready, 2)

    def send_near(c):
        near_copy(IMG, c).start()
        near_copy(TXT, c).start()

    loop(0, chunks, send_near)

    temper = jnp.exp(jnp.full((1, 1), scalars[0, 0], jnp.float32))
    offset = scalars[1, 0]
    sums[...] = jnp.zeros_like(sums)

    def fold(values):
        total = jnp.sum(values.reshape(rows // 8, 8, values.shape[1]), axis=0)
        return sum(total[:, k : k + 128] for k in range(0, values.shape[1], 128))

    def piece(own, slot, start, size, matched=False, loss=False):
        partner = land[slot, start : start + size]
        scores = lax.dot_general(
            land[own], partner, (((1,), (1,)), ((), ())), preferred_element_type=jnp.float32
        )
        logit = temper * scores + offset
        if matched:
            r = lax.broadcasted_iota(jnp.int32, (rows, size), 0)
            c = lax.broadcasted_iota(jnp.int32, (rows, size), 1) + start
            logit = jnp.where(r == c, -logit, logit)
        small = jnp.exp(-jnp.abs(logit))
        recip = 1.0 / (1.0 + small)
        slope = jnp.where(logit >= 0, recip, small * recip)
        if matched:
            slope = jnp.where(r == c, -slope, slope)
        if loss:
            sums[0] += fold(jnp.maximum(logit, 0.0) + jnp.log1p(small))
            sums[1] += fold(slope * scores)
            sums[2] += fold(slope)
        weighted = (temper * slope).astype(jnp.bfloat16)
        direction = jnp.dot(weighted, partner, preferred_element_type=jnp.float32)
        if matched:
            acc[own] = direction
        else:
            acc[own] += direction

    def project_texts(c):
        here = pl.ds(pl.multiple_of(c * PASS, PASS), PASS)
        raw[TXT, here] = project(raw[TXT, here], inverse[TXT, here], acc[TXT, here])

    def hand_on(c):
        wait_arrival(IMG2, c)
        wait_arrival(TXT2, c)
        forward_copy(c).start()

    piece(TXT, IMG, 0, rows, matched=True, loss=True)
    piece(IMG, TXT, 0, rows, matched=True)
    loop(0, chunks, hand_on)
    loop(lead, chunks, lambda c: own_copy(c).start())
    piece(TXT, IMG2, 0, rows, loss=True)
    piece(IMG, TXT2, 0, rows)
    loop(0, chunks, lambda c: wait_arrival(IMG1, c))
    piece(TXT, IMG1, 0, rows, loss=True)

    rows_of = lax.broadcasted_iota(jnp.int32, (8, 128), 0)
    mine = jnp.zeros((8, 128), jnp.float32)
    n_pairs = n_loop * lax.axis_size("group") * rows * rows * (STEPS + 1)
    for k, factor in enumerate((1.0, temper, 1.0)):
        total = jnp.sum(sums[k], axis=0, keepdims=True) * factor / n_pairs
        mine = jnp.where(rows_of == k, jnp.broadcast_to(total, (8, 128)), mine)
    result[...] = mine

    def pair_copy(target, device):
        return pltpu.make_async_remote_copy(
            src_ref=result,
            dst_ref=target,
            send_sem=pair_sem.at[0],
            recv_sem=pair_sem.at[1],
            device_id=device,
            device_id_type=MESH,
        )

    @pl.when(even)
    def _():
        pair_copy(pair_in, above).start()

    @pl.when(odd)
    def _():
        pair_copy(pair_in, below).wait_recv()
        value = result[...] + pair_in[...]
        for tiles, index, size, peer, send, recv in exchanges:
            tiles[index] = value

            def to(k, tiles=tiles, index=index, size=size, peer=peer, send=send, recv=recv):
                return pltpu.make_async_remote_copy(
                    src_ref=tiles.at[index],
                    dst_ref=tiles.at[index],
                    send_sem=send.at[k],
                    recv_sem=recv.at[index],
                    device_id=peer(lax.rem(index + k, size)),
                    device_id_type=MESH,
                )

            for k in range(1, size):
                to(k).start()
            for k in range(1, size):
                source = lax.rem(index + k, size)
                pltpu.make_async_remote_copy(
                    src_ref=tiles.at[source],
                    dst_ref=tiles.at[source],
                    send_sem=send.at[k],
                    recv_sem=recv.at[source],
                    device_id=peer(source),
                    device_id_type=MESH,
                ).wait_recv()
            value = tiles[0]
            for k in range(1, size):
                value = value + tiles[k]
            for k in range(1, size):
                to(k).wait_send()
        result[...] = value
        pltpu.make_async_remote_copy(
            src_ref=result,
            dst_ref=pair_in,
            send_sem=result_sem.at[0],
            recv_sem=result_sem.at[1],
            device_id=below,
            device_id_type=MESH,
        ).start()

    loop(0, rows // PASS, project_texts)

    start = 0
    for size in LAST:
        loop(start // CHUNK, (start + size) // CHUNK, lambda c: wait_arrival(TXT1, c))
        piece(IMG, TXT1, start, size)
        start += size

    back = pltpu.make_async_remote_copy(
        src_ref=result,
        dst_ref=pair_in,
        send_sem=result_sem.at[0],
        recv_sem=result_sem.at[1],
        device_id=below,
        device_id_type=MESH,
    )

    @pl.when(even)
    def _():
        pair_copy(pair_in, above).wait_send()
        back.wait_recv()
        result[...] = pair_in[...]

    @pl.when(odd)
    def _():
        back.wait_send()

    def finish(c):
        own_copy(c).wait_send()
        forward_copy(c).wait_send()
        near_copy(IMG, c).wait_send()
        near_copy(TXT, c).wait_send()

    loop(0, chunks, finish)


def finish_kernel(raw, acc, inverse, result, image_grad, text_grad, summary, stage, totals, sem):
    rows = raw.shape[1]
    steps = rows // PASS
    copies = [pltpu.make_async_copy(raw.at[TXT], text_grad, sem.at[0])]
    copies[0].start()
    for k in range(3):
        totals[k] = jnp.sum(result[k : k + 1, :])
    copies.append(pltpu.make_async_copy(totals, summary, sem.at[1]))
    copies[1].start()
    for c in range(steps):
        here = pl.ds(c * PASS, PASS)
        stage[here] = project(raw[IMG, here], inverse[IMG, here], acc[IMG, here])
        copies.append(pltpu.make_async_copy(stage.at[here], image_grad.at[here], sem.at[2 + c]))
        copies[-1].start()
    for copy in copies:
        copy.wait()


def body(images, texts, log_temp, logit_bias):
    rows, width = images.shape
    chunks = rows // CHUNK
    n_loop = lax.axis_size("loop")
    half = n_loop // 4
    bf16, f32, dma = jnp.bfloat16, jnp.float32, pltpu.SemaphoreType.DMA
    hbm = pl.BlockSpec(memory_space=pltpu.HBM)
    vmem = pl.BlockSpec(memory_space=pltpu.VMEM)
    parts = pl.pallas_call(
        functools.partial(kernel, n_loop),
        out_shape=(
            jax.ShapeDtypeStruct((2, rows, width), bf16),
            jax.ShapeDtypeStruct((2, rows, width), f32),
            jax.ShapeDtypeStruct((2, rows, 1), f32),
            jax.ShapeDtypeStruct((8, 128), f32),
        ),
        in_specs=[hbm] * 4,
        out_specs=(vmem,) * 4,
        scratch_shapes=[
            pltpu.VMEM((6, rows, width), bf16),
            pltpu.SMEM((2, 1), f32),
            pltpu.VMEM((3, 8, 128), f32),
            pltpu.VMEM((8, 128), f32),
            pltpu.VMEM((half, 8, 128), f32),
            pltpu.VMEM((N_Y * N_CORE, 8, 128), f32),
            pltpu.VMEM((4, 8, 128), f32),
            dma((4,)),
            dma((2, chunks)),
            dma((2, chunks)),
            dma((4, chunks)),
            pltpu.SemaphoreType.REGULAR,
            dma((2,)),
            dma((half,)),
            dma((half,)),
            dma((N_Y * N_CORE,)),
            dma((N_Y * N_CORE,)),
            dma((4,)),
            dma((4,)),
            dma((2,)),
        ],
        compiler_params=pltpu.CompilerParams(
            collective_id=0, has_side_effects=True, vmem_limit_bytes=24 * 2**20
        ),
        cost_estimate=pl.CostEstimate(
            flops=24 * rows * rows * width, bytes_accessed=8 * rows * width, transcendentals=2 * 6 * rows * rows
        ),
        name="exchange",
    )(log_temp, logit_bias, images, texts)
    return pl.pallas_call(
        finish_kernel,
        out_shape=(
            jax.ShapeDtypeStruct((rows, width), bf16),
            jax.ShapeDtypeStruct((rows, width), bf16),
            jax.ShapeDtypeStruct((3,), f32),
        ),
        in_specs=[vmem] * 4,
        out_specs=(hbm,) * 3,
        scratch_shapes=[pltpu.VMEM((rows, width), bf16), pltpu.SMEM((3,), f32), dma((2 + rows // PASS,))],
        compiler_params=pltpu.CompilerParams(vmem_limit_bytes=8 * 2**20),
        name="finish",
    )(*parts)


def solution(mesh):
    in_specs = (P(("loop", "group"), None), P(("loop", "group"), None), P(), P())
    out_specs = (P(("loop", "group"), None), P(("loop", "group"), None), P())
    return jax.shard_map(body, mesh=mesh, in_specs=in_specs, out_specs=out_specs, check_vma=False)
```

```python
import functools

import jax
import jax.numpy as jnp
from jax import lax
from jax.experimental import pallas as pl
from jax.experimental.pallas import tpu as pltpu
from jax.sharding import PartitionSpec as P

STEPS = 2
EPS = 1e-06
MESH = pl.DeviceIdType.MESH

CHUNK = 64
LAST = (256, 128, 128)
LEAD = 3
PASS = 256

IMG, TXT, IMG2, TXT2, IMG1, TXT1 = range(6)
N_Y, N_CORE = 4, 2


def project(values, scale, direction):
    unit = values.astype(jnp.float32) * scale
    inner = jnp.sum(unit * direction, axis=1, keepdims=True)
    return ((direction - unit * inner) * scale).astype(jnp.bfloat16)


def kernel(
    n_loop,
    log_temp,
    logit_bias,
    images,
    texts,
    raw,
    acc,
    inverse,
    result,
    land,
    scalars,
    sums,
    mine,
    from_z,
    from_plane,
    load_sem,
    near_send,
    far_send,
    arrived,
    z_ready,
    up_sem,
    z_arrived,
    plane_arrived,
    z_sent,
    plane_sent,
    result_sem,
):
    rows = raw.shape[1]
    chunks = rows // CHUNK
    n_z = n_loop // 2

    p = lax.axis_index("loop")
    h = lax.axis_index("group")
    z, xh = p // 2, lax.rem(p, 2)
    xl, yc = h // (N_Y * N_CORE), lax.rem(h, N_Y * N_CORE)
    odd = lax.rem(z, 2) == 1
    even = lax.rem(z, 2) == 0

    def at(z_, xh_, xl_, yc_):
        return (z_ * 2 + xh_, xl_ * (N_Y * N_CORE) + yc_)

    up = lax.rem(z + 1, n_z)
    down = lax.rem(z + n_z - 1, n_z)
    across = at(z, 1 - xh, xl, yc)
    above = at(up, xh, xl, yc)
    below = at(down, xh, xl, yc)

    spot = (xh * 2 + xl) * (N_Y * N_CORE) + yc
    spots = 4 * N_Y * N_CORE
    is_hub = z == 0
    is_root = jnp.logical_and(is_hub, spot == spots - 1)
    is_branch = jnp.logical_and(is_hub, spot < spots - 1)
    hub = at(0, xh, xl, yc)

    def hub_at(q):
        return at(0, q // (2 * N_Y * N_CORE), lax.rem(q // (N_Y * N_CORE), 2), lax.rem(q, N_Y * N_CORE))

    root = hub_at(spots - 1)

    def loop(start, stop, body):
        def step(i, carry):
            body(i)
            return carry

        lax.fori_loop(start, stop, step, 0)

    barrier = pltpu.get_barrier_semaphore()

    def greet(device):
        pl.semaphore_signal(barrier, inc=1, device_id=device, device_id_type=MESH)

    greet(across)

    @pl.when(even)
    def _():
        greet(above)
        greet(below)

    @pl.when(is_hub)
    def _():
        loop(1, n_z, lambda k: greet(at(k, xh, xl, yc)))

    @pl.when(is_root)
    def _():
        loop(0, spots - 1, lambda q: greet(hub_at(q)))

    first = 1 - xh
    second = xh

    loads = (
        (images, raw.at[IMG]),
        (texts, raw.at[TXT]),
        (log_temp, scalars.at[0]),
        (logit_bias, scalars.at[1]),
    )
    for k, (source, target) in enumerate(loads):
        pltpu.make_async_copy(source, target, load_sem.at[k]).start()
    for k, (source, target) in enumerate(loads):
        pltpu.make_async_copy(source, target, load_sem.at[k]).wait()

    def part(c):
        return pl.ds(pl.multiple_of(c * CHUNK, CHUNK), CHUNK)

    def normalize(block):
        def step(c):
            here = pl.ds(pl.multiple_of(c * PASS, PASS), PASS)
            values = raw[block, here].astype(jnp.float32)
            length = jnp.sqrt(jnp.sum(values * values, axis=1, keepdims=True) + EPS)
            scale = 1.0 / length
            inverse[block, here] = scale
            land[block, here] = (values * scale).astype(jnp.bfloat16)

        loop(0, rows // PASS, step)

    def own_copy(c):
        return pltpu.make_async_remote_copy(
            src_ref=land.at[first, part(c)],
            dst_ref=land.at[4 + first, part(c)],
            send_sem=far_send.at[0, c],
            recv_sem=arrived.at[2 + first, c],
            device_id=across,
            device_id_type=MESH,
        )

    def forward_copy(c):
        return pltpu.make_async_remote_copy(
            src_ref=land.at[2 + xh, part(c)],
            dst_ref=land.at[4 + xh, part(c)],
            send_sem=far_send.at[1, c],
            recv_sem=arrived.at[2 + xh, c],
            device_id=across,
            device_id_type=MESH,
        )

    def near_copy(block, c):
        return pltpu.make_async_remote_copy(
            src_ref=land.at[block, part(c)],
            dst_ref=land.at[2 + block, part(c)],
            send_sem=near_send.at[block, c],
            recv_sem=arrived.at[block, c],
            device_id=below if block == IMG else above,
            device_id_type=MESH,
        )

    def wait_arrival(slot, c):
        pltpu.make_async_remote_copy(
            src_ref=land.at[slot, part(c)],
            dst_ref=land.at[slot, part(c)],
            send_sem=near_send.at[0, 0],
            recv_sem=arrived.at[slot - 2, c],
            device_id=across,
            device_id_type=MESH,
        ).wait_recv()

    normalize(first)

    @pl.when(is_root)
    def _():
        pl.semaphore_wait(barrier, 1)

    @pl.when(jnp.logical_and(even, jnp.logical_not(is_root)))
    def _():
        pl.semaphore_wait(barrier, 2)

    @pl.when(odd)
    def _():
        pl.semaphore_wait(barrier, 4)
        pl.semaphore_signal(z_ready, inc=1, device_id=above, device_id_type=MESH)
        pl.semaphore_signal(z_ready, inc=1, device_id=below, device_id_type=MESH)

    lead = LEAD + xh * (chunks - LEAD)
    loop(0, lead, lambda c: own_copy(c).start())
    normalize(second)

    @pl.when(even)
    def _():
        pl.semaphore_wait(z_ready, 2)

    def send_near(c):
        near_copy(IMG, c).start()
        near_copy(TXT, c).start()

    loop(0, chunks, send_near)

    temper = jnp.exp(jnp.full((1, 1), scalars[0, 0], jnp.float32))
    offset = scalars[1, 0]
    sums[...] = jnp.zeros_like(sums)

    def fold(values):
        total = jnp.sum(values.reshape(rows // 8, 8, values.shape[1]), axis=0)
        return sum(total[:, k : k + 128] for k in range(0, values.shape[1], 128))

    def piece(own, slot, start, size, matched=False, loss=False):
        partner = land[slot, start : start + size]
        scores = lax.dot_general(
            land[own], partner, (((1,), (1,)), ((), ())), preferred_element_type=jnp.float32
        )
        logit = temper * scores + offset
        if matched:
            r = lax.broadcasted_iota(jnp.int32, (rows, size), 0)
            c = lax.broadcasted_iota(jnp.int32, (rows, size), 1) + start
            logit = jnp.where(r == c, -logit, logit)
        small = jnp.exp(-jnp.abs(logit))
        recip = 1.0 / (1.0 + small)
        slope = jnp.where(logit >= 0, recip, small * recip)
        if matched:
            slope = jnp.where(r == c, -slope, slope)
        if loss:
            sums[0] += fold(jnp.maximum(logit, 0.0) + jnp.log1p(small))
            sums[1] += fold(slope * scores)
            sums[2] += fold(slope)
        weighted = (temper * slope).astype(jnp.bfloat16)
        direction = jnp.dot(weighted, partner, preferred_element_type=jnp.float32)
        if matched:
            acc[own] = direction
        else:
            acc[own] += direction

    def project_texts(c):
        here = pl.ds(pl.multiple_of(c * PASS, PASS), PASS)
        raw[TXT, here] = project(raw[TXT, here], inverse[TXT, here], acc[TXT, here])

    def hand_on(c):
        wait_arrival(IMG2, c)
        wait_arrival(TXT2, c)
        forward_copy(c).start()

    piece(TXT, IMG, 0, rows, matched=True, loss=True)
    piece(IMG, TXT, 0, rows, matched=True)
    loop(0, chunks, hand_on)
    loop(lead, chunks, lambda c: own_copy(c).start())
    piece(TXT, IMG2, 0, rows, loss=True)
    piece(IMG, TXT2, 0, rows)
    loop(0, chunks, lambda c: wait_arrival(IMG1, c))
    piece(TXT, IMG1, 0, rows, loss=True)

    rows_of = lax.broadcasted_iota(jnp.int32, (8, 128), 0)
    partial = jnp.zeros((8, 128), jnp.float32)
    n_pairs = n_loop * lax.axis_size("group") * rows * rows * (STEPS + 1)
    for k, factor in enumerate((1.0, temper, 1.0)):
        total = jnp.sum(sums[k], axis=0, keepdims=True) * factor / n_pairs
        partial = jnp.where(rows_of == k, jnp.broadcast_to(total, (8, 128)), partial)
    mine[...] = partial

    def to_hub(k):
        return pltpu.make_async_remote_copy(
            src_ref=mine,
            dst_ref=from_z.at[k],
            send_sem=up_sem,
            recv_sem=z_arrived.at[k],
            device_id=hub,
            device_id_type=MESH,
        )

    def to_root(q):
        return pltpu.make_async_remote_copy(
            src_ref=mine,
            dst_ref=from_plane.at[q],
            send_sem=up_sem,
            recv_sem=plane_arrived.at[q],
            device_id=root,
            device_id_type=MESH,
        )

    def to_plane(q):
        return pltpu.make_async_remote_copy(
            src_ref=result,
            dst_ref=result,
            send_sem=plane_sent.at[q],
            recv_sem=result_sem,
            device_id=hub_at(q),
            device_id_type=MESH,
        )

    def to_line(k):
        return pltpu.make_async_remote_copy(
            src_ref=result,
            dst_ref=result,
            send_sem=z_sent.at[k],
            recv_sem=result_sem,
            device_id=at(k, xh, xl, yc),
            device_id_type=MESH,
        )

    def reduce_at_hub():
        loop(1, n_z, lambda k: to_hub(k).wait_recv())
        mine[...] += jnp.sum(from_z[1:], axis=0)

        @pl.when(is_branch)
        def _():
            to_root(spot).start()
            to_plane(spot).wait_recv()

        @pl.when(is_root)
        def _():
            loop(0, spots - 1, lambda q: to_root(q).wait_recv())
            result[...] = mine[...] + jnp.sum(from_plane[: spots - 1], axis=0)
            loop(0, spots - 1, lambda q: to_plane(q).start())

        loop(1, n_z, lambda k: to_line(k).start())

    @pl.when(jnp.logical_not(is_hub))
    def _():
        to_hub(z).start()

    loop(0, rows // PASS, project_texts)

    start = 0
    for k, size in enumerate(LAST):
        if k == len(LAST) - 1:
            pl.when(is_hub)(reduce_at_hub)
        loop(start // CHUNK, (start + size) // CHUNK, lambda c: wait_arrival(TXT1, c))
        piece(IMG, TXT1, start, size)
        start += size

    @pl.when(jnp.logical_not(is_hub))
    def _():
        to_hub(z).wait_send()
        to_line(z).wait_recv()

    @pl.when(is_branch)
    def _():
        to_root(spot).wait_send()

    @pl.when(is_root)
    def _():
        loop(0, spots - 1, lambda q: to_plane(q).wait_send())

    @pl.when(is_hub)
    def _():
        loop(1, n_z, lambda k: to_line(k).wait_send())

    def finish(c):
        own_copy(c).wait_send()
        forward_copy(c).wait_send()
        near_copy(IMG, c).wait_send()
        near_copy(TXT, c).wait_send()

    loop(0, chunks, finish)


def finish_kernel(raw, acc, inverse, result, image_grad, text_grad, summary, stage, totals, sem):
    rows = raw.shape[1]
    steps = rows // PASS
    copies = [pltpu.make_async_copy(raw.at[TXT], text_grad, sem.at[0])]
    copies[0].start()
    for k in range(3):
        totals[k] = jnp.sum(result[k : k + 1, :])
    copies.append(pltpu.make_async_copy(totals, summary, sem.at[1]))
    copies[1].start()
    for c in range(steps):
        here = pl.ds(c * PASS, PASS)
        stage[here] = project(raw[IMG, here], inverse[IMG, here], acc[IMG, here])
        copies.append(pltpu.make_async_copy(stage.at[here], image_grad.at[here], sem.at[2 + c]))
        copies[-1].start()
    for copy in copies:
        copy.wait()


def body(images, texts, log_temp, logit_bias):
    rows, width = images.shape
    chunks = rows // CHUNK
    n_loop = lax.axis_size("loop")
    n_z, spots = n_loop // 2, 4 * N_Y * N_CORE
    bf16, f32, dma = jnp.bfloat16, jnp.float32, pltpu.SemaphoreType.DMA
    hbm = pl.BlockSpec(memory_space=pltpu.HBM)
    vmem = pl.BlockSpec(memory_space=pltpu.VMEM)
    parts = pl.pallas_call(
        functools.partial(kernel, n_loop),
        out_shape=(
            jax.ShapeDtypeStruct((2, rows, width), bf16),
            jax.ShapeDtypeStruct((2, rows, width), f32),
            jax.ShapeDtypeStruct((2, rows, 1), f32),
            jax.ShapeDtypeStruct((8, 128), f32),
        ),
        in_specs=[hbm] * 4,
        out_specs=(vmem,) * 4,
        scratch_shapes=[
            pltpu.VMEM((6, rows, width), bf16),
            pltpu.SMEM((2, 1), f32),
            pltpu.VMEM((3, 8, 128), f32),
            pltpu.VMEM((8, 128), f32),
            pltpu.VMEM((n_z, 8, 128), f32),
            pltpu.VMEM((spots, 8, 128), f32),
            dma((4,)),
            dma((2, chunks)),
            dma((2, chunks)),
            dma((4, chunks)),
            pltpu.SemaphoreType.REGULAR,
            dma(()),
            dma((n_z,)),
            dma((spots,)),
            dma((n_z,)),
            dma((spots,)),
            dma(()),
        ],
        compiler_params=pltpu.CompilerParams(
            collective_id=0, has_side_effects=True, vmem_limit_bytes=24 * 2**20
        ),
        cost_estimate=pl.CostEstimate(
            flops=24 * rows * rows * width, bytes_accessed=8 * rows * width, transcendentals=2 * 6 * rows * rows
        ),
        name="exchange",
    )(log_temp, logit_bias, *(pltpu.with_memory_space_constraint(a, pltpu.HBM) for a in (images, texts)))
    return pl.pallas_call(
        finish_kernel,
        out_shape=(
            jax.ShapeDtypeStruct((rows, width), bf16),
            jax.ShapeDtypeStruct((rows, width), bf16),
            jax.ShapeDtypeStruct((3,), f32),
        ),
        in_specs=[vmem] * 4,
        out_specs=(hbm,) * 3,
        scratch_shapes=[pltpu.VMEM((rows, width), bf16), pltpu.SMEM((3,), f32), dma((2 + rows // PASS,))],
        compiler_params=pltpu.CompilerParams(vmem_limit_bytes=8 * 2**20),
        name="finish",
    )(*parts)


def solution(mesh):
    in_specs = (P(("loop", "group"), None), P(("loop", "group"), None), P(), P())
    out_specs = (P(("loop", "group"), None), P(("loop", "group"), None), P())
    return jax.shard_map(body, mesh=mesh, in_specs=in_specs, out_specs=out_specs, check_vma=False)
```

```python
import functools

import jax
import jax.numpy as jnp
from jax import lax
from jax.experimental import pallas as pl
from jax.experimental.pallas import tpu as pltpu
from jax.sharding import PartitionSpec as P

STEPS = 2
EPS = 1e-06
MESH = pl.DeviceIdType.MESH

CHUNK = 32
LAST = (256, 128, 128)
LEAD = 4
PASS = 256

IMG, TXT, IMG2, TXT2, IMG1, TXT1 = range(6)
N_Y, N_CORE = 4, 2


def project(values, scale, direction):
    unit = values.astype(jnp.float32) * scale
    inner = jnp.sum(unit * direction, axis=1, keepdims=True)
    return ((direction - unit * inner) * scale).astype(jnp.bfloat16)


def kernel(
    n_loop,
    log_temp,
    logit_bias,
    images,
    texts,
    raw,
    acc,
    inverse,
    result,
    land,
    sums,
    tiles_z,
    tiles_g,
    tiles_x,
    load_sem,
    near_send,
    far_send,
    arrived,
    z_ready,
    group_ready,
    z_send,
    z_recv,
    g_send,
    g_recv,
    x_send,
    x_recv,
):
    rows = raw.shape[1]
    chunks = rows // CHUNK
    n_z = n_loop // 2

    p = lax.axis_index("loop")
    h = lax.axis_index("group")
    z, xh = p // 2, lax.rem(p, 2)
    xl, yc = h // (N_Y * N_CORE), lax.rem(h, N_Y * N_CORE)
    odd = lax.rem(z, 2) == 1
    even = lax.rem(z, 2) == 0

    def at(z_, xh_, xl_, yc_):
        return (z_ * 2 + xh_, xl_ * (N_Y * N_CORE) + yc_)

    up = lax.rem(z + 1, n_z)
    down = lax.rem(z + n_z - 1, n_z)
    across = at(z, 1 - xh, xl, yc)
    above = at(up, xh, xl, yc)
    below = at(down, xh, xl, yc)

    def z_peer(i):
        return at(i, xh, xl, yc)

    def g_peer(i):
        return at(z, xh, xl, i)

    def x_peer(i):
        return at(z, i // 2, lax.rem(i, 2), yc)

    groups = (
        (tiles_z, z, n_z, n_z - 1, z_peer, z_send, z_recv),
        (tiles_g, yc, N_Y * N_CORE, 0, g_peer, g_send, g_recv),
        (tiles_x, xh * 2 + xl, 4, 0, x_peer, x_send, x_recv),
    )

    def loop(start, stop, body):
        def step(i, carry):
            body(i)
            return carry

        lax.fori_loop(start, stop, step, 0)

    barrier = pltpu.get_barrier_semaphore()

    def greet(device):
        pl.semaphore_signal(barrier, inc=1, device_id=device, device_id_type=MESH)

    greet(across)

    @pl.when(even)
    def _():
        greet(above)
        greet(below)

    expected = 1 + 2 * lax.rem(z, 2)
    for _, place, size, collector, peer, _, _ in groups:
        expected = expected + jnp.where(place == collector, size - 1, 0)
        pl.when(place != collector)(functools.partial(greet, peer(collector)))

    first = 1 - xh
    second = xh

    loads = (
        (images, raw.at[IMG]),
        (texts, raw.at[TXT]),
    )
    for k, (source, target) in enumerate(loads):
        pltpu.make_async_copy(source, target, load_sem.at[k]).start()
    for k, (source, target) in enumerate(loads):
        pltpu.make_async_copy(source, target, load_sem.at[k]).wait()

    def part(c):
        return pl.ds(pl.multiple_of(c * CHUNK, CHUNK), CHUNK)

    def normalize(block):
        def step(c):
            here = pl.ds(pl.multiple_of(c * PASS, PASS), PASS)
            values = raw[block, here].astype(jnp.float32)
            length = jnp.sqrt(jnp.sum(values * values, axis=1, keepdims=True) + EPS)
            scale = 1.0 / length
            inverse[block, here] = scale
            land[block, here] = (values * scale).astype(jnp.bfloat16)

        loop(0, rows // PASS, step)

    def own_copy(c):
        return pltpu.make_async_remote_copy(
            src_ref=land.at[first, part(c)],
            dst_ref=land.at[4 + first, part(c)],
            send_sem=far_send.at[0, c],
            recv_sem=arrived.at[2 + first, c],
            device_id=across,
            device_id_type=MESH,
        )

    def forward_copy(c):
        return pltpu.make_async_remote_copy(
            src_ref=land.at[2 + xh, part(c)],
            dst_ref=land.at[4 + xh, part(c)],
            send_sem=far_send.at[1, c],
            recv_sem=arrived.at[2 + xh, c],
            device_id=across,
            device_id_type=MESH,
        )

    def near_copy(block, c):
        return pltpu.make_async_remote_copy(
            src_ref=land.at[block, part(c)],
            dst_ref=land.at[2 + block, part(c)],
            send_sem=near_send.at[block, c],
            recv_sem=arrived.at[block, c],
            device_id=below if block == IMG else above,
            device_id_type=MESH,
        )

    def wait_arrival(slot, c):
        pltpu.make_async_remote_copy(
            src_ref=land.at[slot, part(c)],
            dst_ref=land.at[slot, part(c)],
            send_sem=near_send.at[0, 0],
            recv_sem=arrived.at[slot - 2, c],
            device_id=across,
            device_id_type=MESH,
        ).wait_recv()

    normalize(first)

    pl.semaphore_wait(barrier, expected)

    @pl.when(odd)
    def _():
        pl.semaphore_signal(z_ready.at[1], inc=1, device_id=above, device_id_type=MESH)
        pl.semaphore_signal(z_ready.at[0], inc=1, device_id=below, device_id_type=MESH)

    lead = LEAD + xh * (chunks - LEAD)
    loop(0, lead, lambda c: own_copy(c).start())
    normalize(second)

    for block in (TXT, IMG):
        pl.when(even)(functools.partial(pl.semaphore_wait, z_ready.at[0 if block == TXT else 1], 1))
        loop(0, chunks, lambda c: near_copy(block, c).start())

    for k, (_, place, size, collector, peer, _, _) in enumerate(groups):

        @pl.when(place == collector)
        def _():
            def tell(i):
                device = peer(lax.rem(collector + i, size))
                pl.semaphore_signal(group_ready.at[k], inc=1, device_id=device, device_id_type=MESH)

            loop(1, size, tell)

    temper = jnp.exp(log_temp[...].reshape(1, 1))
    offset = logit_bias[...].reshape(1, 1)
    sums[...] = jnp.zeros_like(sums)

    def fold(values):
        total = jnp.sum(values.reshape(rows // 8, 8, values.shape[1]), axis=0)
        return sum(total[:, k : k + 128] for k in range(0, values.shape[1], 128))

    def piece(own, slot, start, size, matched=False, loss=False):
        partner = land[slot, start : start + size]
        scores = lax.dot_general(
            land[own], partner, (((1,), (1,)), ((), ())), preferred_element_type=jnp.float32
        )
        logit = temper * scores + offset
        if matched:
            r = lax.broadcasted_iota(jnp.int32, (rows, size), 0)
            c = lax.broadcasted_iota(jnp.int32, (rows, size), 1) + start
            logit = jnp.where(r == c, -logit, logit)
        small = jnp.exp(-jnp.abs(logit))
        recip = 1.0 / (1.0 + small)
        slope = jnp.where(logit >= 0, recip, small * recip)
        if matched:
            slope = jnp.where(r == c, -slope, slope)
        if loss:
            sums[0] += fold(jnp.maximum(logit, 0.0) + jnp.log1p(small))
            sums[1] += fold(slope * scores)
            sums[2] += fold(slope)
        weighted = (temper * slope).astype(jnp.bfloat16)
        direction = jnp.dot(weighted, partner, preferred_element_type=jnp.float32)
        if matched:
            acc[own] = direction
        else:
            acc[own] += direction

    def project_texts(c):
        here = pl.ds(pl.multiple_of(c * PASS, PASS), PASS)
        raw[TXT, here] = project(raw[TXT, here], inverse[TXT, here], acc[TXT, here])

    def hand_on(c):
        wait_arrival(2 + xh, c)
        forward_copy(c).start()

    loop(0, 2, hand_on)
    piece(TXT, IMG, 0, rows, matched=True, loss=True)
    loop(2, 4, hand_on)
    piece(IMG, TXT, 0, rows, matched=True)
    loop(4, chunks, hand_on)
    loop(lead, chunks, lambda c: own_copy(c).start())
    loop(0, chunks, lambda c: wait_arrival(3 - xh, c))
    piece(TXT, IMG2, 0, rows, loss=True)
    piece(IMG, TXT2, 0, rows)
    loop(0, chunks, lambda c: wait_arrival(IMG1, c))
    piece(TXT, IMG1, 0, rows, loss=True)

    rows_of = lax.broadcasted_iota(jnp.int32, (8, 128), 0)
    partial = jnp.zeros((8, 128), jnp.float32)
    n_pairs = n_loop * lax.axis_size("group") * rows * rows * (STEPS + 1)
    for k, factor in enumerate((1.0, temper, 1.0)):
        total = jnp.sum(sums[k], axis=0, keepdims=True) * factor / n_pairs
        partial = jnp.where(rows_of == k, jnp.broadcast_to(total, (8, 128)), partial)

    def exchange_copy(group, k):
        tiles, place, size, _, peer, send, recv = group
        return pltpu.make_async_remote_copy(
            src_ref=tiles.at[place],
            dst_ref=tiles.at[place],
            send_sem=send.at[k],
            recv_sem=recv.at[place],
            device_id=peer(lax.rem(place + k, size)),
            device_id_type=MESH,
        )

    def exchange_start(k, value):
        tiles, place, size, collector, _, _, _ = groups[k]
        tiles[place] = value
        pl.when(place != collector)(functools.partial(pl.semaphore_wait, group_ready.at[k], 1))
        loop(1, size, lambda i: exchange_copy(groups[k], i).start())

    def exchange_end(k):
        tiles, place, size, _, peer, send, recv = groups[k]

        def wait(i):
            source = lax.rem(place + i, size)
            pltpu.make_async_remote_copy(
                src_ref=tiles.at[source],
                dst_ref=tiles.at[source],
                send_sem=send.at[i],
                recv_sem=recv.at[source],
                device_id=peer(source),
                device_id_type=MESH,
            ).wait_recv()

        loop(1, size, wait)
        return jnp.sum(tiles[...], axis=0)

    exchange_start(0, partial)
    loop(0, rows // PASS, project_texts)

    start = 0
    for k, size in enumerate(LAST):
        if k:
            exchange_start(k, exchange_end(k - 1))
        loop(start // CHUNK, (start + size) // CHUNK, lambda c: wait_arrival(TXT1, c))
        piece(IMG, TXT1, start, size)
        start += size

    result[...] = exchange_end(2)
    for group in groups:
        loop(1, group[2], lambda i, group=group: exchange_copy(group, i).wait_send())

    def finish(c):
        own_copy(c).wait_send()
        forward_copy(c).wait_send()
        near_copy(IMG, c).wait_send()
        near_copy(TXT, c).wait_send()

    loop(0, chunks, finish)


def finish_kernel(raw, acc, inverse, result, image_grad, text_grad, summary, stage, totals, sem):
    rows = raw.shape[1]
    steps = rows // PASS
    copies = [pltpu.make_async_copy(raw.at[TXT], text_grad, sem.at[0])]
    copies[0].start()
    for k in range(3):
        totals[k] = jnp.sum(result[k : k + 1, :])
    copies.append(pltpu.make_async_copy(totals, summary, sem.at[1]))
    copies[1].start()
    for c in range(steps):
        here = pl.ds(c * PASS, PASS)
        stage[here] = project(raw[IMG, here], inverse[IMG, here], acc[IMG, here])
        copies.append(pltpu.make_async_copy(stage.at[here], image_grad.at[here], sem.at[2 + c]))
        copies[-1].start()
    for copy in copies:
        copy.wait()


def body(images, texts, log_temp, logit_bias):
    rows, width = images.shape
    chunks = rows // CHUNK
    n_loop = lax.axis_size("loop")
    n_z = n_loop // 2
    bf16, f32, dma = jnp.bfloat16, jnp.float32, pltpu.SemaphoreType.DMA
    hbm = pl.BlockSpec(memory_space=pltpu.HBM)
    vmem = pl.BlockSpec(memory_space=pltpu.VMEM)
    parts = pl.pallas_call(
        functools.partial(kernel, n_loop),
        out_shape=(
            jax.ShapeDtypeStruct((2, rows, width), bf16),
            jax.ShapeDtypeStruct((2, rows, width), f32),
            jax.ShapeDtypeStruct((2, rows, 1), f32),
            jax.ShapeDtypeStruct((8, 128), f32),
        ),
        in_specs=[vmem, vmem, hbm, hbm],
        out_specs=(vmem,) * 4,
        scratch_shapes=[
            pltpu.VMEM((6, rows, width), bf16),
            pltpu.VMEM((3, 8, 128), f32),
            pltpu.VMEM((n_z, 8, 128), f32),
            pltpu.VMEM((N_Y * N_CORE, 8, 128), f32),
            pltpu.VMEM((4, 8, 128), f32),
            dma((2,)),
            dma((2, chunks)),
            dma((2, chunks)),
            dma((4, chunks)),
            pltpu.SemaphoreType.REGULAR((2,)),
            pltpu.SemaphoreType.REGULAR((3,)),
            dma((n_z,)),
            dma((n_z,)),
            dma((N_Y * N_CORE,)),
            dma((N_Y * N_CORE,)),
            dma((4,)),
            dma((4,)),
        ],
        compiler_params=pltpu.CompilerParams(
            collective_id=0, has_side_effects=True, vmem_limit_bytes=24 * 2**20
        ),
        cost_estimate=pl.CostEstimate(
            flops=24 * rows * rows * width, bytes_accessed=8 * rows * width, transcendentals=2 * 6 * rows * rows
        ),
        name="exchange",
    )(log_temp, logit_bias, *(pltpu.with_memory_space_constraint(a, pltpu.HBM) for a in (images, texts)))
    return pl.pallas_call(
        finish_kernel,
        out_shape=(
            jax.ShapeDtypeStruct((rows, width), bf16),
            jax.ShapeDtypeStruct((rows, width), bf16),
            jax.ShapeDtypeStruct((3,), f32),
        ),
        in_specs=[vmem] * 4,
        out_specs=(hbm,) * 3,
        scratch_shapes=[pltpu.VMEM((rows, width), bf16), pltpu.SMEM((3,), f32), dma((2 + rows // PASS,))],
        compiler_params=pltpu.CompilerParams(vmem_limit_bytes=8 * 2**20),
        name="finish",
    )(*parts)


def solution(mesh):
    in_specs = (P(("loop", "group"), None), P(("loop", "group"), None), P(), P())
    out_specs = (P(("loop", "group"), None), P(("loop", "group"), None), P())
    return jax.shard_map(body, mesh=mesh, in_specs=in_specs, out_specs=out_specs, check_vma=False)
```

```python
import functools

import jax
import jax.numpy as jnp
from jax import lax
from jax.experimental import pallas as pl
from jax.experimental.pallas import tpu as pltpu
from jax.sharding import PartitionSpec as P

STEPS = 2
EPS = 1e-06
MESH = pl.DeviceIdType.MESH

CHUNK = 32
LAST = (256, 128, 128)
LEAD = 5
PASS = 256

IMG, TXT, IMG2, TXT2, IMG1, TXT1 = range(6)
N_Y, N_CORE = 4, 2


def project(values, scale, direction):
    unit = values.astype(jnp.float32) * scale
    inner = jnp.sum(unit * direction, axis=1, keepdims=True)
    return ((direction - unit * inner) * scale).astype(jnp.bfloat16)


def kernel(
    n_loop,
    log_temp,
    logit_bias,
    images,
    texts,
    raw,
    acc,
    inverse,
    result,
    land,
    sums,
    tiles_z,
    tiles_g,
    tiles_x,
    load_sem,
    near_send,
    far_send,
    arrived,
    z_ready,
    group_ready,
    z_send,
    z_recv,
    g_send,
    g_recv,
    x_send,
    x_recv,
):
    rows = raw.shape[1]
    chunks = rows // CHUNK
    n_z = n_loop // 2

    p = lax.axis_index("loop")
    h = lax.axis_index("group")
    z, xh = p // 2, lax.rem(p, 2)
    xl, yc = h // (N_Y * N_CORE), lax.rem(h, N_Y * N_CORE)
    odd = lax.rem(z, 2) == 1
    even = lax.rem(z, 2) == 0

    def at(z_, xh_, xl_, yc_):
        return (z_ * 2 + xh_, xl_ * (N_Y * N_CORE) + yc_)

    up = lax.rem(z + 1, n_z)
    down = lax.rem(z + n_z - 1, n_z)
    across = at(z, 1 - xh, xl, yc)
    above = at(up, xh, xl, yc)
    below = at(down, xh, xl, yc)

    def z_peer(i):
        return at(i, xh, xl, yc)

    def g_peer(i):
        return at(z, xh, xl, i)

    def x_peer(i):
        return at(z, i // 2, lax.rem(i, 2), yc)

    groups = (
        (tiles_z, z, n_z, n_z - 1, z_peer, z_send, z_recv),
        (tiles_g, yc, N_Y * N_CORE, 0, g_peer, g_send, g_recv),
        (tiles_x, xh * 2 + xl, 4, 0, x_peer, x_send, x_recv),
    )

    def loop(start, stop, body):
        def step(i, carry):
            body(i)
            return carry

        lax.fori_loop(start, stop, step, 0)

    barrier = pltpu.get_barrier_semaphore()

    def greet(device):
        pl.semaphore_signal(barrier, inc=1, device_id=device, device_id_type=MESH)

    greet(across)

    @pl.when(even)
    def _():
        greet(above)
        greet(below)

    expected = 1 + 2 * lax.rem(z, 2)
    for _, place, size, collector, peer, _, _ in groups:
        expected = expected + jnp.where(place == collector, size - 1, 0)
        pl.when(place != collector)(functools.partial(greet, peer(collector)))

    first = 1 - xh

    loads = (
        (images, raw.at[IMG]),
        (texts, raw.at[TXT]),
    )
    for k, (source, target) in enumerate(loads):
        pltpu.make_async_copy(source, target, load_sem.at[k]).start()
    for k, (source, target) in enumerate(loads):
        pltpu.make_async_copy(source, target, load_sem.at[k]).wait()

    def part(c):
        return pl.ds(pl.multiple_of(c * CHUNK, CHUNK), CHUNK)

    def normalize(block):
        def step(c):
            here = pl.ds(pl.multiple_of(c * PASS, PASS), PASS)
            values = raw[block, here].astype(jnp.float32)
            length = jnp.sqrt(jnp.sum(values * values, axis=1, keepdims=True) + EPS)
            scale = 1.0 / length
            inverse[block, here] = scale
            land[block, here] = (values * scale).astype(jnp.bfloat16)

        loop(0, rows // PASS, step)

    def own_copy(c):
        return pltpu.make_async_remote_copy(
            src_ref=land.at[first, part(c)],
            dst_ref=land.at[4 + first, part(c)],
            send_sem=far_send.at[0, c],
            recv_sem=arrived.at[2 + first, c],
            device_id=across,
            device_id_type=MESH,
        )

    def forward_copy(c):
        return pltpu.make_async_remote_copy(
            src_ref=land.at[2 + xh, part(c)],
            dst_ref=land.at[4 + xh, part(c)],
            send_sem=far_send.at[1, c],
            recv_sem=arrived.at[2 + xh, c],
            device_id=across,
            device_id_type=MESH,
        )

    def near_copy(block, c):
        return pltpu.make_async_remote_copy(
            src_ref=land.at[block, part(c)],
            dst_ref=land.at[2 + block, part(c)],
            send_sem=near_send.at[block, c],
            recv_sem=arrived.at[block, c],
            device_id=below if block == IMG else above,
            device_id_type=MESH,
        )

    def wait_arrival(slot, c):
        pltpu.make_async_remote_copy(
            src_ref=land.at[slot, part(c)],
            dst_ref=land.at[slot, part(c)],
            send_sem=near_send.at[0, 0],
            recv_sem=arrived.at[slot - 2, c],
            device_id=across,
            device_id_type=MESH,
        ).wait_recv()

    normalize(IMG)
    normalize(TXT)
    pl.semaphore_wait(barrier, expected)

    @pl.when(odd)
    def _():
        pl.semaphore_signal(z_ready.at[1], inc=1, device_id=above, device_id_type=MESH)
        pl.semaphore_signal(z_ready.at[0], inc=1, device_id=below, device_id_type=MESH)

    loop(0, LEAD, lambda c: own_copy(c).start())
    pl.when(even)(functools.partial(pl.semaphore_wait, z_ready.at[1], 1))
    loop(0, chunks, lambda c: near_copy(IMG, c).start())
    pl.when(xh == 1)(lambda: loop(LEAD, chunks, lambda c: own_copy(c).start()))
    pl.when(even)(functools.partial(pl.semaphore_wait, z_ready.at[0], 1))
    loop(0, chunks, lambda c: near_copy(TXT, c).start())

    for k, (_, place, size, collector, peer, _, _) in enumerate(groups):

        @pl.when(place == collector)
        def _():
            def tell(i):
                device = peer(lax.rem(collector + i, size))
                pl.semaphore_signal(group_ready.at[k], inc=1, device_id=device, device_id_type=MESH)

            loop(1, size, tell)

    temper = jnp.exp(log_temp[...].reshape(1, 1))
    offset = logit_bias[...].reshape(1, 1)
    sums[...] = jnp.zeros_like(sums)

    def fold(values):
        total = jnp.sum(values.reshape(rows // 8, 8, values.shape[1]), axis=0)
        return sum(total[:, k : k + 128] for k in range(0, values.shape[1], 128))

    def piece(own, slot, start, size, matched=False, loss=False):
        partner = land[slot, start : start + size]
        scores = lax.dot_general(
            land[own], partner, (((1,), (1,)), ((), ())), preferred_element_type=jnp.float32
        )
        logit = temper * scores + offset
        if matched:
            r = lax.broadcasted_iota(jnp.int32, (rows, size), 0)
            c = lax.broadcasted_iota(jnp.int32, (rows, size), 1) + start
            logit = jnp.where(r == c, -logit, logit)
        small = jnp.exp(-jnp.abs(logit))
        recip = 1.0 / (1.0 + small)
        slope = jnp.where(logit >= 0, recip, small * recip)
        if matched:
            slope = jnp.where(r == c, -slope, slope)
        if loss:
            sums[0] += fold(jnp.maximum(logit, 0.0) + jnp.log1p(small))
            sums[1] += fold(slope * scores)
            sums[2] += fold(slope)
        weighted = (temper * slope).astype(jnp.bfloat16)
        direction = jnp.dot(weighted, partner, preferred_element_type=jnp.float32)
        if matched:
            acc[own] = direction
        else:
            acc[own] += direction

    def project_texts(c):
        here = pl.ds(pl.multiple_of(c * PASS, PASS), PASS)
        raw[TXT, here] = project(raw[TXT, here], inverse[TXT, here], acc[TXT, here])

    def hand_on(c):
        wait_arrival(2 + xh, c)
        forward_copy(c).start()

    def piece_of(own, slot, start, size, **kinds):
        if slot in (IMG1, TXT1):
            loop(start // CHUNK, (start + size) // CHUNK, lambda c: wait_arrival(slot, c))
        piece(own, slot, start, size, **kinds)

    def rest(c):
        wait_arrival(3 - xh, c)

    part_rows = rows // 2
    middle = chunks // 2
    loop(0, 2, hand_on)
    piece(TXT, IMG, 0, rows, matched=True, loss=True)
    loop(2, 4, hand_on)
    piece(IMG, TXT, 0, rows, matched=True)
    loop(4, middle, hand_on)
    loop(0, middle, rest)
    piece(TXT, IMG2, 0, part_rows, loss=True)
    loop(middle, middle + 4, hand_on)
    piece_of(TXT, IMG1, 0, part_rows, loss=True)
    loop(middle + 4, chunks, hand_on)
    pl.when(xh == 0)(lambda: loop(LEAD, chunks, lambda c: own_copy(c).start()))
    loop(middle, chunks, rest)
    piece(TXT, IMG2, part_rows, part_rows, loss=True)
    piece_of(TXT, IMG1, part_rows, part_rows, loss=True)

    lane = lax.broadcasted_iota(jnp.int32, (1, 128), 1)
    partial = jnp.zeros((1, 128), jnp.float32)
    n_pairs = n_loop * lax.axis_size("group") * rows * rows * (STEPS + 1)
    for k, factor in enumerate((1.0, temper, 1.0)):
        total = jnp.sum(jnp.sum(sums[k], axis=0, keepdims=True), axis=1, keepdims=True) * factor / n_pairs
        partial = jnp.where(lane == k, total, partial)

    def exchange_copy(group, k):
        tiles, place, size, _, peer, send, recv = group
        return pltpu.make_async_remote_copy(
            src_ref=tiles.at[place],
            dst_ref=tiles.at[place],
            send_sem=send.at[k],
            recv_sem=recv.at[place],
            device_id=peer(lax.rem(place + k, size)),
            device_id_type=MESH,
        )

    def exchange_start(k, value):
        tiles, place, size, collector, _, _, _ = groups[k]
        tiles[place] = value
        pl.when(place != collector)(functools.partial(pl.semaphore_wait, group_ready.at[k], 1))
        for i in sorted(range(1, size), key=lambda i: -min(i, size - i)):
            exchange_copy(groups[k], i).start()

    def exchange_end(k):
        tiles, place, size, _, peer, send, recv = groups[k]

        def wait(i):
            source = lax.rem(place + i, size)
            pltpu.make_async_remote_copy(
                src_ref=tiles.at[source],
                dst_ref=tiles.at[source],
                send_sem=send.at[i],
                recv_sem=recv.at[source],
                device_id=peer(source),
                device_id_type=MESH,
            ).wait_recv()

        loop(1, size, wait)
        return jnp.sum(tiles[...], axis=0)

    exchange_start(0, partial)
    piece(IMG, TXT2, 0, rows)
    loop(0, rows // PASS, project_texts)

    def sent_early(c):
        near_copy(IMG, c).wait_send()
        near_copy(TXT, c).wait_send()

        @pl.when(c < LEAD)
        def _():
            own_copy(c).wait_send()

    start = 0
    for k, size in enumerate(LAST):
        if k:
            exchange_start(k, exchange_end(k - 1))
        if k == len(LAST) - 1:
            loop(0, chunks, sent_early)
        piece_of(IMG, TXT1, start, size)
        start += size

    result[...] = exchange_end(2)
    for group in groups:
        loop(1, group[2], lambda i, group=group: exchange_copy(group, i).wait_send())

    loop(LEAD, chunks, lambda c: own_copy(c).wait_send())
    loop(0, chunks, lambda c: forward_copy(c).wait_send())


def finish_kernel(raw, acc, inverse, result, image_grad, text_grad, summary, stage, totals, sem):
    rows = raw.shape[1]
    steps = rows // PASS
    copies = [pltpu.make_async_copy(raw.at[TXT], text_grad, sem.at[0])]
    copies[0].start()
    lane = lax.broadcasted_iota(jnp.int32, (1, 128), 1)
    for k in range(3):
        totals[k] = jnp.sum(jnp.where(lane == k, result[...], 0.0))
    copies.append(pltpu.make_async_copy(totals, summary, sem.at[1]))
    copies[1].start()
    for c in range(steps):
        here = pl.ds(c * PASS, PASS)
        stage[here] = project(raw[IMG, here], inverse[IMG, here], acc[IMG, here])
        copies.append(pltpu.make_async_copy(stage.at[here], image_grad.at[here], sem.at[2 + c]))
        copies[-1].start()
    for copy in copies:
        copy.wait()


def body(images, texts, log_temp, logit_bias):
    rows, width = images.shape
    chunks = rows // CHUNK
    n_loop = lax.axis_size("loop")
    n_z = n_loop // 2
    bf16, f32, dma = jnp.bfloat16, jnp.float32, pltpu.SemaphoreType.DMA
    hbm = pl.BlockSpec(memory_space=pltpu.HBM)
    vmem = pl.BlockSpec(memory_space=pltpu.VMEM)
    parts = pl.pallas_call(
        functools.partial(kernel, n_loop),
        out_shape=(
            jax.ShapeDtypeStruct((2, rows, width), bf16),
            jax.ShapeDtypeStruct((2, rows, width), f32),
            jax.ShapeDtypeStruct((2, rows, 1), f32),
            jax.ShapeDtypeStruct((1, 128), f32),
        ),
        in_specs=[vmem, vmem, hbm, hbm],
        out_specs=(vmem,) * 4,
        scratch_shapes=[
            pltpu.VMEM((6, rows, width), bf16),
            pltpu.VMEM((3, 8, 128), f32),
            pltpu.VMEM((n_z, 1, 128), f32),
            pltpu.VMEM((N_Y * N_CORE, 1, 128), f32),
            pltpu.VMEM((4, 1, 128), f32),
            dma((2,)),
            dma((2, chunks)),
            dma((2, chunks)),
            dma((4, chunks)),
            pltpu.SemaphoreType.REGULAR((2,)),
            pltpu.SemaphoreType.REGULAR((3,)),
            dma((n_z,)),
            dma((n_z,)),
            dma((N_Y * N_CORE,)),
            dma((N_Y * N_CORE,)),
            dma((4,)),
            dma((4,)),
        ],
        compiler_params=pltpu.CompilerParams(
            collective_id=0, has_side_effects=True, vmem_limit_bytes=24 * 2**20
        ),
        cost_estimate=pl.CostEstimate(
            flops=24 * rows * rows * width, bytes_accessed=8 * rows * width, transcendentals=2 * 6 * rows * rows
        ),
        name="exchange",
    )(log_temp, logit_bias, *(pltpu.with_memory_space_constraint(a, pltpu.HBM) for a in (images, texts)))
    return pl.pallas_call(
        finish_kernel,
        out_shape=(
            jax.ShapeDtypeStruct((rows, width), bf16),
            jax.ShapeDtypeStruct((rows, width), bf16),
            jax.ShapeDtypeStruct((3,), f32),
        ),
        in_specs=[vmem] * 4,
        out_specs=(hbm,) * 3,
        scratch_shapes=[pltpu.VMEM((rows, width), bf16), pltpu.SMEM((3,), f32), dma((2 + rows // PASS,))],
        compiler_params=pltpu.CompilerParams(vmem_limit_bytes=8 * 2**20),
        name="finish",
    )(*parts)


def solution(mesh):
    in_specs = (P(("loop", "group"), None), P(("loop", "group"), None), P(), P())
    out_specs = (P(("loop", "group"), None), P(("loop", "group"), None), P())
    return jax.shard_map(body, mesh=mesh, in_specs=in_specs, out_specs=out_specs, check_vma=False)
```

```python
import functools

import jax
import jax.numpy as jnp
from jax import lax
from jax.experimental import pallas as pl
from jax.experimental.pallas import tpu as pltpu
from jax.sharding import PartitionSpec as P

STEPS = 2
EPS = 1e-06
MESH = pl.DeviceIdType.MESH

CHUNK = 32
LAST = (256, 128, 128)
LEAD = 4
LEAD_FIRST = 8
PASS = 256

IMG, TXT, IMG2, TXT2, IMG1, TXT1 = range(6)
N_Y, N_CORE = 4, 2


def project(values, scale, direction):
    unit = values.astype(jnp.float32) * scale
    inner = jnp.sum(unit * direction, axis=1, keepdims=True)
    return ((direction - unit * inner) * scale).astype(jnp.bfloat16)


def kernel(
    n_loop,
    log_temp,
    logit_bias,
    images,
    texts,
    raw,
    result,
    acc,
    inverse,
    land,
    sums,
    tiles_z,
    tiles_p,
    load_sem,
    near_send,
    far_send,
    arrived,
    z_ready,
    relayed,
    group_ready,
    z_send,
    z_recv,
    p_send,
    p_recv,
):
    rows = raw.shape[1]
    chunks = rows // CHUNK
    n_z = n_loop // 2

    p = lax.axis_index("loop")
    h = lax.axis_index("group")
    z, xh = p // 2, lax.rem(p, 2)
    xl, yc = h // (N_Y * N_CORE), lax.rem(h, N_Y * N_CORE)
    odd = lax.rem(z, 2) == 1
    even = lax.rem(z, 2) == 0

    def at(z_, xh_, xl_, yc_):
        return (z_ * 2 + xh_, xl_ * (N_Y * N_CORE) + yc_)

    up = lax.rem(z + 1, n_z)
    down = lax.rem(z + n_z - 1, n_z)
    across = at(z, 1 - xh, xl, yc)
    above = at(up, xh, xl, yc)
    below = at(down, xh, xl, yc)

    def z_peer(i):
        return at(i, xh, xl, yc)

    def plane_peer(i):
        return at(z, i // (2 * N_Y * N_CORE), lax.rem(i // (N_Y * N_CORE), 2), lax.rem(i, N_Y * N_CORE))

    spots = 4 * N_Y * N_CORE
    groups = (
        (tiles_z, z, n_z, n_z - 5, z_peer, z_send, z_recv),
        (tiles_p, (xh * 2 + xl) * (N_Y * N_CORE) + yc, spots, spots - 1, plane_peer, p_send, p_recv),
    )

    def loop(start, stop, body):
        def step(i, carry):
            body(i)
            return carry

        lax.fori_loop(start, stop, step, 0)

    barrier = pltpu.get_barrier_semaphore()

    def greet(device):
        pl.semaphore_signal(barrier, inc=1, device_id=device, device_id_type=MESH)

    greet(across)

    @pl.when(even)
    def _():
        greet(above)
        greet(below)

    expected = 1 + 2 * lax.rem(z, 2)
    for _, place, size, collector, peer, _, _ in groups[1:]:
        expected = expected + jnp.where(place == collector, size - 1, 0)
        pl.when(place != collector)(functools.partial(greet, peer(collector)))

    last, collector = n_z - 1, n_z - 5
    expected = expected + jnp.where(z == last, n_z - 6, jnp.where(z == collector, 4, 0))
    near_collector = jnp.logical_and(z >= collector - 4, z < collector)
    pl.when(near_collector)(lambda: greet(z_peer(collector)))
    pl.when(jnp.logical_or(z < collector - 4, jnp.logical_and(z > collector, z < last)))(lambda: greet(z_peer(last)))

    first = 1 - xh

    loads = (
        (images, raw.at[IMG]),
        (texts, raw.at[TXT]),
    )
    for k, (source, target) in enumerate(loads):
        pltpu.make_async_copy(source, target, load_sem.at[k]).start()
    for k, (source, target) in enumerate(loads):
        pltpu.make_async_copy(source, target, load_sem.at[k]).wait()

    def part(c):
        return pl.ds(pl.multiple_of(c * CHUNK, CHUNK), CHUNK)

    def normalize(block):
        def step(c):
            here = pl.ds(pl.multiple_of(c * PASS, PASS), PASS)
            values = raw[block, here].astype(jnp.float32)
            length = jnp.sqrt(jnp.sum(values * values, axis=1, keepdims=True) + EPS)
            scale = 1.0 / length
            inverse[block, here] = scale
            land[block, here] = (values * scale).astype(jnp.bfloat16)

        loop(0, rows // PASS, step)

    def own_copy(c):
        return pltpu.make_async_remote_copy(
            src_ref=land.at[first, part(c)],
            dst_ref=land.at[4 + first, part(c)],
            send_sem=far_send.at[0],
            recv_sem=arrived.at[2 + first, c],
            device_id=across,
            device_id_type=MESH,
        )

    def forward_copy(c):
        return pltpu.make_async_remote_copy(
            src_ref=land.at[2 + xh, part(c)],
            dst_ref=land.at[4 + xh, part(c)],
            send_sem=far_send.at[1],
            recv_sem=arrived.at[2 + xh, c],
            device_id=across,
            device_id_type=MESH,
        )

    def near_copy(block, c):
        return pltpu.make_async_remote_copy(
            src_ref=land.at[block, part(c)],
            dst_ref=land.at[2 + block, part(c)],
            send_sem=near_send.at[block],
            recv_sem=arrived.at[block, c],
            device_id=below if block == IMG else above,
            device_id_type=MESH,
        )

    def wait_arrival(slot, c):
        pltpu.make_async_remote_copy(
            src_ref=land.at[slot, part(c)],
            dst_ref=land.at[slot, part(c)],
            send_sem=near_send.at[0],
            recv_sem=arrived.at[slot - 2, c],
            device_id=across,
            device_id_type=MESH,
        ).wait_recv()

    normalize(IMG)
    normalize(TXT)
    pl.semaphore_wait(barrier, expected)

    @pl.when(odd)
    def _():
        pl.semaphore_signal(z_ready.at[1], inc=1, device_id=above, device_id_type=MESH)
        pl.semaphore_signal(z_ready.at[0], inc=1, device_id=below, device_id_type=MESH)

    lead = jnp.where(z == 0, LEAD_FIRST, LEAD)
    loop(0, lead, lambda c: own_copy(c).start())

    @pl.when(z == last)
    def _():
        pl.semaphore_signal(relayed.at[0], inc=1, device_id=z_peer(collector + 1), device_id_type=MESH)

    pl.when(even)(functools.partial(pl.semaphore_wait, z_ready.at[1], 1))
    loop(0, chunks, lambda c: near_copy(IMG, c).start())
    pl.when(xh == 1)(lambda: loop(lead, chunks, lambda c: own_copy(c).start()))
    pl.when(even)(functools.partial(pl.semaphore_wait, z_ready.at[0], 1))
    loop(0, chunks, lambda c: near_copy(TXT, c).start())

    def tell_group(k):
        _, place, size, collector, peer, _, _ = groups[k]

        def tell(i):
            device = peer(lax.rem(collector + i, size))
            pl.semaphore_signal(group_ready.at[k], inc=1, device_id=device, device_id_type=MESH)

        pl.when(place == collector)(lambda: loop(1, size, tell))

    temper = jnp.exp(log_temp[...].reshape(1, 1))
    offset = logit_bias[...].reshape(1, 1)
    sums[...] = jnp.zeros_like(sums)

    def fold(values):
        total = jnp.sum(values.reshape(rows // 8, 8, values.shape[1]), axis=0)
        return sum(total[:, k : k + 128] for k in range(0, values.shape[1], 128))

    def piece(own, slot, start, size, matched=False, loss=False):
        partner = land[slot, start : start + size]
        scores = lax.dot_general(
            land[own], partner, (((1,), (1,)), ((), ())), preferred_element_type=jnp.float32
        )
        logit = temper * scores + offset
        if matched:
            r = lax.broadcasted_iota(jnp.int32, (rows, size), 0)
            c = lax.broadcasted_iota(jnp.int32, (rows, size), 1) + start
            logit = jnp.where(r == c, -logit, logit)
        small = jnp.exp(-jnp.abs(logit))
        recip = 1.0 / (1.0 + small)
        slope = jnp.where(logit >= 0, recip, small * recip)
        if matched:
            slope = jnp.where(r == c, -slope, slope)
        if loss:
            sums[0] += fold(jnp.maximum(logit, 0.0) + jnp.log1p(small))
            sums[1] += fold(slope * scores)
            sums[2] += fold(slope)
        weighted = (temper * slope).astype(jnp.bfloat16)
        direction = jnp.dot(weighted, partner, preferred_element_type=jnp.float32)
        if matched:
            acc[own] = direction
        else:
            acc[own] += direction

    def project_block(block, c):
        here = pl.ds(pl.multiple_of(c * PASS, PASS), PASS)
        raw[block, here] = project(raw[block, here], inverse[block, here], acc[block, here])

    def hand_on(c):
        wait_arrival(2 + xh, c)
        forward_copy(c).start()

    def piece_of(own, slot, start, size, **kinds):
        if slot in (IMG1, TXT1):
            loop(start // CHUNK, (start + size) // CHUNK, lambda c: wait_arrival(slot, c))
        piece(own, slot, start, size, **kinds)

    def rest(c):
        wait_arrival(3 - xh, c)

    part_rows = rows // 2
    middle = chunks // 2
    loop(0, 2, hand_on)
    piece(TXT, IMG, 0, rows, matched=True, loss=True)
    loop(2, 4, hand_on)

    @pl.when(z == collector + 1)
    def _():
        pl.semaphore_wait(relayed.at[0], 1)
        pl.semaphore_signal(relayed.at[1], inc=1, device_id=z_peer(collector), device_id_type=MESH)

    piece(IMG, TXT, 0, rows, matched=True)
    loop(4, middle, hand_on)
    pl.when(z == collector)(functools.partial(pl.semaphore_wait, relayed.at[1], 1))
    for k in range(len(groups)):
        tell_group(k)
    pl.when(xh == 1)(lambda: loop(0, middle, rest))
    piece(TXT, IMG2, 0, part_rows, loss=True)
    loop(middle, middle + 4, hand_on)
    piece_of(TXT, IMG1, 0, part_rows, loss=True)
    loop(middle + 4, chunks, hand_on)
    pl.when(xh == 0)(lambda: loop(lead, chunks, lambda c: own_copy(c).start()))
    pl.when(xh == 1)(lambda: loop(middle, chunks, rest))
    piece(TXT, IMG2, part_rows, part_rows, loss=True)
    piece_of(TXT, IMG1, part_rows, part_rows // 2, loss=True)
    piece_of(TXT, IMG1, part_rows + part_rows // 2, part_rows // 2, loss=True)

    lane = lax.broadcasted_iota(jnp.int32, (1, 128), 1)
    partial = jnp.zeros((1, 128), jnp.float32)
    n_pairs = n_loop * lax.axis_size("group") * rows * rows * (STEPS + 1)
    for k, factor in enumerate((1.0, temper, 1.0)):
        total = jnp.sum(jnp.sum(sums[k], axis=0, keepdims=True), axis=1, keepdims=True) * factor / n_pairs
        partial = jnp.where(lane == k, total, partial)

    def exchange_copy(k, source, target, device):
        tiles, _, _, _, _, send, recv = groups[k]
        return pltpu.make_async_remote_copy(
            src_ref=tiles.at[source],
            dst_ref=tiles.at[target],
            send_sem=send,
            recv_sem=recv,
            device_id=device,
            device_id_type=MESH,
        )

    def exchange_start(k, value):
        tiles, place, size, collector, peer, _, _ = groups[k]
        tiles[place] = value
        pl.when(place != collector)(functools.partial(pl.semaphore_wait, group_ready.at[k], 1))
        for i in sorted(range(1, size), key=lambda i: -min(i, size - i)):
            exchange_copy(k, place, place, peer(lax.rem(place + i, size))).start()

    def exchange_end(k):
        tiles, _, size, _, _, _, _ = groups[k]
        others = pl.ds(0, size - 1)
        exchange_copy(k, others, others, across).wait_recv()
        return jnp.sum(tiles[...], axis=0)

    def exchange_sent(k):
        others = pl.ds(0, groups[k][2] - 1)
        exchange_copy(k, others, others, across).wait_send()

    exchange_start(0, partial)
    pl.when(xh == 0)(lambda: loop(0, chunks, rest))
    piece(IMG, TXT2, 0, rows)
    loop(0, rows // PASS, functools.partial(project_block, TXT))

    def all_sent(semaphore):
        pltpu.make_async_remote_copy(
            src_ref=land.at[IMG],
            dst_ref=land.at[IMG2],
            send_sem=semaphore,
            recv_sem=arrived.at[0, 0],
            device_id=across,
            device_id_type=MESH,
        ).wait_send()

    start = 0
    for k, size in enumerate(LAST):
        if k == 1:
            exchange_start(1, exchange_end(0))
        if k == len(LAST) - 1:
            all_sent(near_send.at[IMG])
            all_sent(near_send.at[TXT])
        piece_of(IMG, TXT1, start, size)
        start += size

    loop(0, rows // PASS, functools.partial(project_block, IMG))
    result[...] = exchange_end(1)
    exchange_sent(0)
    exchange_sent(1)
    all_sent(far_send.at[0])
    all_sent(far_send.at[1])


def finish_kernel(raw, result, image_grad, text_grad, summary, totals, sem):
    copies = [
        pltpu.make_async_copy(raw.at[IMG], image_grad, sem.at[0]),
        pltpu.make_async_copy(raw.at[TXT], text_grad, sem.at[1]),
        pltpu.make_async_copy(totals, summary, sem.at[2]),
    ]
    copies[0].start()
    copies[1].start()
    lane = lax.broadcasted_iota(jnp.int32, (1, 128), 1)
    for k in range(3):
        totals[k] = jnp.sum(jnp.where(lane == k, result[...], 0.0))
    copies[2].start()
    for copy in copies:
        copy.wait()


def body(images, texts, log_temp, logit_bias):
    rows, width = images.shape
    chunks = rows // CHUNK
    n_loop = lax.axis_size("loop")
    n_z, spots = n_loop // 2, 4 * N_Y * N_CORE
    bf16, f32, dma = jnp.bfloat16, jnp.float32, pltpu.SemaphoreType.DMA
    hbm = pl.BlockSpec(memory_space=pltpu.HBM)
    vmem = pl.BlockSpec(memory_space=pltpu.VMEM)
    raw, result = pl.pallas_call(
        functools.partial(kernel, n_loop),
        out_shape=(
            jax.ShapeDtypeStruct((2, rows, width), bf16),
            jax.ShapeDtypeStruct((1, 128), f32),
        ),
        in_specs=[vmem, vmem, hbm, hbm],
        out_specs=(vmem,) * 2,
        scratch_shapes=[
            pltpu.VMEM((2, rows, width), f32),
            pltpu.VMEM((2, rows, 1), f32),
            pltpu.VMEM((6, rows, width), bf16),
            pltpu.VMEM((3, 8, 128), f32),
            pltpu.VMEM((n_z, 1, 128), f32),
            pltpu.VMEM((spots, 1, 128), f32),
            dma((2,)),
            dma((2,)),
            dma((2,)),
            dma((4, chunks)),
            pltpu.SemaphoreType.REGULAR((2,)),
            pltpu.SemaphoreType.REGULAR((2,)),
            pltpu.SemaphoreType.REGULAR((2,)),
            dma(()),
            dma(()),
            dma(()),
            dma(()),
        ],
        compiler_params=pltpu.CompilerParams(
            collective_id=0, has_side_effects=True, vmem_limit_bytes=24 * 2**20
        ),
        cost_estimate=pl.CostEstimate(
            flops=24 * rows * rows * width, bytes_accessed=8 * rows * width, transcendentals=2 * 6 * rows * rows
        ),
        name="exchange",
    )(log_temp, logit_bias, *(pltpu.with_memory_space_constraint(a, pltpu.HBM) for a in (images, texts)))
    return pl.pallas_call(
        finish_kernel,
        out_shape=(
            jax.ShapeDtypeStruct((rows, width), bf16),
            jax.ShapeDtypeStruct((rows, width), bf16),
            jax.ShapeDtypeStruct((3,), f32),
        ),
        in_specs=[vmem] * 2,
        out_specs=(hbm,) * 3,
        scratch_shapes=[pltpu.SMEM((3,), f32), dma((3,))],
        compiler_params=pltpu.CompilerParams(vmem_limit_bytes=8 * 2**20),
        name="finish",
    )(raw, result)


def solution(mesh):
    in_specs = (P(("loop", "group"), None), P(("loop", "group"), None), P(), P())
    out_specs = (P(("loop", "group"), None), P(("loop", "group"), None), P())
    return jax.shard_map(body, mesh=mesh, in_specs=in_specs, out_specs=out_specs, check_vma=False)
```

```python
import functools

import jax
import jax.numpy as jnp
from jax import lax
from jax.experimental import pallas as pl
from jax.experimental.pallas import tpu as pltpu
from jax.sharding import PartitionSpec as P

STEPS = 2
EPS = 1e-06
MESH = pl.DeviceIdType.MESH

CHUNK = 32
LAST = (256, 128, 128)
LEAD = 3
HELD = 2
LEAD_FIRST = 8
PASS = 256

IMG, TXT, IMG2, TXT2, IMG1, TXT1 = range(6)
N_Y, N_CORE = 4, 2


def project(values, scale, direction):
    unit = values.astype(jnp.float32) * scale
    inner = jnp.sum(unit * direction, axis=1, keepdims=True)
    return ((direction - unit * inner) * scale).astype(jnp.bfloat16)


def kernel(
    n_loop,
    log_temp,
    logit_bias,
    images,
    texts,
    raw,
    result,
    acc,
    inverse,
    land,
    sums,
    tiles_z,
    tiles_p,
    load_sem,
    near_send,
    far_send,
    arrived,
    z_ready,
    relayed,
    group_ready,
    z_send,
    z_recv,
    p_send,
    p_recv,
):
    rows = raw.shape[1]
    chunks = rows // CHUNK
    n_z = n_loop // 2

    loads = [
        pltpu.make_async_copy(source, raw.at[block], load_sem.at[block])
        for block, source in ((IMG, images), (TXT, texts))
    ]
    for load in loads:
        load.start()

    p = lax.axis_index("loop")
    h = lax.axis_index("group")
    z, xh = p // 2, lax.rem(p, 2)
    xl, yc = h // (N_Y * N_CORE), lax.rem(h, N_Y * N_CORE)

    def at(z_, xh_, xl_, yc_):
        return (z_ * 2 + xh_, xl_ * (N_Y * N_CORE) + yc_)

    up = lax.rem(z + 1, n_z)
    down = lax.rem(z + n_z - 1, n_z)
    across = at(z, 1 - xh, xl, yc)
    above = at(up, xh, xl, yc)
    below = at(down, xh, xl, yc)

    def z_peer(i):
        return at(i, xh, xl, yc)

    def plane_peer(i):
        return at(z, i // (2 * N_Y * N_CORE), lax.rem(i // (N_Y * N_CORE), 2), lax.rem(i, N_Y * N_CORE))

    spots = 4 * N_Y * N_CORE
    groups = (
        (tiles_z, z, n_z, n_z - 5, z_peer, z_send, z_recv),
        (tiles_p, (xh * 2 + xl) * (N_Y * N_CORE) + yc, spots, spots - 1, plane_peer, p_send, p_recv),
    )

    def loop(start, stop, body):
        def step(i, carry):
            body(i)
            return carry

        lax.fori_loop(start, stop, step, 0)

    barrier = pltpu.get_barrier_semaphore()

    def greet(device):
        pl.semaphore_signal(barrier, inc=1, device_id=device, device_id_type=MESH)

    last, collector = n_z - 1, n_z - 5
    greet(across)
    greet(below)
    pl.when(z != last)(lambda: greet(above))
    expected = 3 - jnp.where(z == 0, 1, 0)
    _, place, size, hearer, peer, _, _ = groups[1]
    expected = expected + jnp.where(place == hearer, size - 1, 0)
    pl.when(place != hearer)(functools.partial(greet, peer(hearer)))

    expected = expected + jnp.where(z == last, n_z - 6, jnp.where(z == collector, 4, 0))
    near_collector = jnp.logical_and(z >= collector - 4, z < collector)
    pl.when(near_collector)(lambda: greet(z_peer(collector)))
    pl.when(jnp.logical_or(z < collector - 4, jnp.logical_and(z > collector, z < last)))(lambda: greet(z_peer(last)))

    first = 1 - xh

    def part(c):
        return pl.ds(pl.multiple_of(c * CHUNK, CHUNK), CHUNK)

    def normalize(block):
        def step(c):
            here = pl.ds(pl.multiple_of(c * PASS, PASS), PASS)
            values = raw[block, here].astype(jnp.float32)
            length = jnp.sqrt(jnp.sum(values * values, axis=1, keepdims=True) + EPS)
            scale = 1.0 / length
            inverse[block, here] = scale
            land[block, here] = (values * scale).astype(jnp.bfloat16)

        loop(0, rows // PASS, step)

    def own_copy(c):
        return pltpu.make_async_remote_copy(
            src_ref=land.at[first, part(c)],
            dst_ref=land.at[4 + first, part(c)],
            send_sem=far_send.at[0],
            recv_sem=arrived.at[2 + first, c],
            device_id=across,
            device_id_type=MESH,
        )

    def forward_copy(c):
        return pltpu.make_async_remote_copy(
            src_ref=land.at[2 + xh, part(c)],
            dst_ref=land.at[4 + xh, part(c)],
            send_sem=far_send.at[1],
            recv_sem=arrived.at[2 + xh, c],
            device_id=across,
            device_id_type=MESH,
        )

    def near_copy(block, c):
        return pltpu.make_async_remote_copy(
            src_ref=land.at[block, part(c)],
            dst_ref=land.at[2 + block, part(c)],
            send_sem=near_send.at[block],
            recv_sem=arrived.at[block, c],
            device_id=below if block == IMG else above,
            device_id_type=MESH,
        )

    def wait_arrival(slot, c):
        pltpu.make_async_remote_copy(
            src_ref=land.at[slot, part(c)],
            dst_ref=land.at[slot, part(c)],
            send_sem=near_send.at[0],
            recv_sem=arrived.at[slot - 2, c],
            device_id=across,
            device_id_type=MESH,
        ).wait_recv()

    for block in (IMG, TXT):
        loads[block].wait()
        normalize(block)
    pl.semaphore_wait(barrier, expected)

    @pl.when(z == last)
    def _():
        pl.semaphore_signal(z_ready, inc=1, device_id=above, device_id_type=MESH)

    lead = jnp.where(z == 0, LEAD_FIRST, LEAD)
    loop(0, lead, lambda c: own_copy(c).start())

    @pl.when(z == last)
    def _():
        pl.semaphore_signal(relayed.at[0], inc=1, device_id=z_peer(collector + 1), device_id_type=MESH)

    pl.when(z == 0)(functools.partial(pl.semaphore_wait, z_ready, 1))
    loop(0, chunks, lambda c: near_copy(IMG, c).start())
    pl.when(xh == 1)(lambda: loop(lead, chunks, lambda c: own_copy(c).start()))
    loop(0, chunks, lambda c: near_copy(TXT, c).start())

    def tell_group(k):
        _, place, size, collector, peer, _, _ = groups[k]

        def tell(i):
            device = peer(lax.rem(collector + i, size))
            pl.semaphore_signal(group_ready.at[k], inc=1, device_id=device, device_id_type=MESH)

        pl.when(place == collector)(lambda: loop(1, size, tell))

    temper = jnp.exp(log_temp[...].reshape(1, 1))
    offset = logit_bias[...].reshape(1, 1)
    sums[...] = jnp.zeros_like(sums)

    def fold(values):
        total = jnp.sum(values.reshape(rows // 8, 8, values.shape[1]), axis=0)
        return sum(total[:, k : k + 128] for k in range(0, values.shape[1], 128))

    def piece(own, slot, start, size, matched=False, loss=False, after_loss=None):
        partner = land[slot, start : start + size]
        scores = lax.dot_general(
            land[own], partner, (((1,), (1,)), ((), ())), preferred_element_type=jnp.float32
        )
        logit = temper * scores + offset
        if matched:
            r = lax.broadcasted_iota(jnp.int32, (rows, size), 0)
            c = lax.broadcasted_iota(jnp.int32, (rows, size), 1) + start
            logit = jnp.where(r == c, -logit, logit)
        small = jnp.exp(-jnp.abs(logit))
        recip = 1.0 / (1.0 + small)
        slope = jnp.where(logit >= 0, recip, small * recip)
        if matched:
            slope = jnp.where(r == c, -slope, slope)
        if loss:
            sums[0] += fold(jnp.maximum(logit, 0.0) + jnp.log1p(small))
            sums[1] += fold(slope * scores)
            sums[2] += fold(slope)
        if after_loss:
            after_loss()
        weighted = (temper * slope).astype(jnp.bfloat16)
        direction = jnp.dot(weighted, partner, preferred_element_type=jnp.float32)
        if matched:
            acc[own] = direction
        else:
            acc[own] += direction

    def project_block(block, c):
        here = pl.ds(pl.multiple_of(c * PASS, PASS), PASS)
        raw[block, here] = project(raw[block, here], inverse[block, here], acc[block, here])

    def hand_on(c):
        wait_arrival(2 + xh, c)
        forward_copy(c).start()

    def piece_of(own, slot, start, size, **kinds):
        if slot in (IMG1, TXT1):
            loop(start // CHUNK, (start + size) // CHUNK, lambda c: wait_arrival(slot, c))
        piece(own, slot, start, size, **kinds)

    def rest(c):
        wait_arrival(3 - xh, c)

    part_rows = rows // 2
    middle = chunks // 2
    loop(0, 2, hand_on)
    piece(TXT, IMG, 0, rows, matched=True, loss=True)
    loop(2, 4, hand_on)

    @pl.when(z == collector + 1)
    def _():
        pl.semaphore_wait(relayed.at[0], 1)
        pl.semaphore_signal(relayed.at[1], inc=1, device_id=z_peer(collector), device_id_type=MESH)

    piece(IMG, TXT, 0, rows, matched=True)
    loop(4, middle, hand_on)
    pl.when(z == collector)(functools.partial(pl.semaphore_wait, relayed.at[1], 1))
    for k in range(len(groups)):
        tell_group(k)
    pl.when(xh == 1)(lambda: loop(0, middle, rest))
    piece(TXT, IMG2, 0, part_rows, loss=True)
    loop(middle, middle + 4, hand_on)
    piece_of(TXT, IMG1, 0, part_rows, loss=True)
    loop(middle + 4, chunks - HELD, hand_on)
    loop(chunks - HELD, chunks, lambda c: wait_arrival(2 + xh, c))

    @pl.when(xh == 0)
    def _():
        loop(chunks - HELD, chunks, lambda c: forward_copy(c).start())
        loop(lead, chunks - HELD, lambda c: own_copy(c).start())

    pl.when(xh == 1)(lambda: loop(middle, chunks, rest))
    piece(TXT, IMG2, part_rows, part_rows, loss=True)
    piece_of(TXT, IMG1, part_rows, part_rows // 2, loss=True)
    def sums_of_device():
        lane = lax.broadcasted_iota(jnp.int32, (1, 128), 1)
        partial = jnp.zeros((1, 128), jnp.float32)
        n_pairs = n_loop * lax.axis_size("group") * rows * rows * (STEPS + 1)
        for k, factor in enumerate((1.0, temper, 1.0)):
            total = jnp.sum(jnp.sum(sums[k], axis=0, keepdims=True), axis=1, keepdims=True) * factor / n_pairs
            partial = jnp.where(lane == k, total, partial)
        return partial

    def exchange_copy(k, source, target, device):
        tiles, _, _, _, _, send, recv = groups[k]
        return pltpu.make_async_remote_copy(
            src_ref=tiles.at[source],
            dst_ref=tiles.at[target],
            send_sem=send,
            recv_sem=recv,
            device_id=device,
            device_id_type=MESH,
        )

    def line_order():
        steps = sorted(range(1, n_z), key=lambda i: -min(i, n_z - i))
        return [z_peer(lax.rem(z + i, n_z)) for i in steps]

    def plane_order():
        x, y, core = xh * 2 + xl, yc // N_CORE, lax.rem(yc, N_CORE)
        columns = [lax.rem(x + i, 4) for i in (2, 1, 3, 0)]
        columns = [(z * 2 + c // 2, lax.rem(c, 2) * (N_Y * N_CORE)) for c in columns]
        spots_y = [lax.rem(y + i, N_Y) * N_CORE for i in (2, 1, 3, 0)]
        spots_of = [s + lax.rem(core + i, N_CORE) for s in spots_y for i in (1, 0)]
        return [(at_loop, at_group + s) for at_loop, at_group in columns for s in spots_of][:-1]

    def exchange_start(k, value):
        tiles, place, _, collector, _, _, _ = groups[k]
        tiles[place] = value
        pl.when(place != collector)(functools.partial(pl.semaphore_wait, group_ready.at[k], 1))
        for device in line_order() if k == 0 else plane_order():
            exchange_copy(k, place, place, device).start()

    def exchange_end(k):
        tiles, _, size, _, _, _, _ = groups[k]
        others = pl.ds(0, size - 1)
        exchange_copy(k, others, others, across).wait_recv()
        return jnp.sum(tiles[...], axis=0)

    def exchange_sent(k):
        others = pl.ds(0, groups[k][2] - 1)
        exchange_copy(k, others, others, across).wait_send()

    piece_of(
        TXT,
        IMG1,
        part_rows + part_rows // 2,
        part_rows // 2,
        loss=True,
        after_loss=lambda: exchange_start(0, sums_of_device()),
    )
    pl.when(xh == 0)(lambda: loop(0, chunks, rest))
    piece(IMG, TXT2, 0, rows)
    loop(0, rows // PASS, functools.partial(project_block, TXT))

    def all_sent(semaphore):
        pltpu.make_async_remote_copy(
            src_ref=land.at[IMG],
            dst_ref=land.at[IMG2],
            send_sem=semaphore,
            recv_sem=arrived.at[0, 0],
            device_id=across,
            device_id_type=MESH,
        ).wait_send()

    start = 0
    for k, size in enumerate(LAST):
        if k == 1:
            exchange_start(1, exchange_end(0))
            pl.when(xh == 0)(lambda: loop(chunks - HELD, chunks, lambda c: own_copy(c).start()))
            pl.when(xh == 1)(lambda: loop(chunks - HELD, chunks, lambda c: forward_copy(c).start()))
        if k == len(LAST) - 1:
            all_sent(near_send.at[IMG])
            all_sent(near_send.at[TXT])
        piece_of(IMG, TXT1, start, size)
        start += size

    loop(0, rows // PASS, functools.partial(project_block, IMG))
    result[...] = exchange_end(1)
    exchange_sent(0)
    exchange_sent(1)
    all_sent(far_send.at[0])
    all_sent(far_send.at[1])


def finish_kernel(raw, result, image_grad, text_grad, summary, totals, sem):
    copies = [
        pltpu.make_async_copy(raw.at[IMG], image_grad, sem.at[0]),
        pltpu.make_async_copy(raw.at[TXT], text_grad, sem.at[1]),
        pltpu.make_async_copy(totals, summary, sem.at[2]),
    ]
    copies[0].start()
    copies[1].start()
    lane = lax.broadcasted_iota(jnp.int32, (1, 128), 1)
    for k in range(3):
        totals[k] = jnp.sum(jnp.where(lane == k, result[...], 0.0))
    copies[2].start()
    for copy in copies:
        copy.wait()


def body(images, texts, log_temp, logit_bias):
    rows, width = images.shape
    chunks = rows // CHUNK
    n_loop = lax.axis_size("loop")
    n_z, spots = n_loop // 2, 4 * N_Y * N_CORE
    bf16, f32, dma = jnp.bfloat16, jnp.float32, pltpu.SemaphoreType.DMA
    hbm = pl.BlockSpec(memory_space=pltpu.HBM)
    vmem = pl.BlockSpec(memory_space=pltpu.VMEM)
    raw, result = pl.pallas_call(
        functools.partial(kernel, n_loop),
        out_shape=(
            jax.ShapeDtypeStruct((2, rows, width), bf16),
            jax.ShapeDtypeStruct((1, 128), f32),
        ),
        in_specs=[vmem, vmem, hbm, hbm],
        out_specs=(vmem,) * 2,
        scratch_shapes=[
            pltpu.VMEM((2, rows, width), f32),
            pltpu.VMEM((2, rows, 1), f32),
            pltpu.VMEM((6, rows, width), bf16),
            pltpu.VMEM((3, 8, 128), f32),
            pltpu.VMEM((n_z, 1, 128), f32),
            pltpu.VMEM((spots, 1, 128), f32),
            dma((2,)),
            dma((2,)),
            dma((2,)),
            dma((4, chunks)),
            pltpu.SemaphoreType.REGULAR,
            pltpu.SemaphoreType.REGULAR((2,)),
            pltpu.SemaphoreType.REGULAR((2,)),
            dma(()),
            dma(()),
            dma(()),
            dma(()),
        ],
        compiler_params=pltpu.CompilerParams(
            collective_id=0, has_side_effects=True, vmem_limit_bytes=24 * 2**20
        ),
        cost_estimate=pl.CostEstimate(
            flops=24 * rows * rows * width, bytes_accessed=8 * rows * width, transcendentals=2 * 6 * rows * rows
        ),
        name="exchange",
    )(log_temp, logit_bias, *(pltpu.with_memory_space_constraint(a, pltpu.HBM) for a in (images, texts)))
    return pl.pallas_call(
        finish_kernel,
        out_shape=(
            jax.ShapeDtypeStruct((rows, width), bf16),
            jax.ShapeDtypeStruct((rows, width), bf16),
            jax.ShapeDtypeStruct((3,), f32),
        ),
        in_specs=[vmem] * 2,
        out_specs=(hbm,) * 3,
        scratch_shapes=[pltpu.SMEM((3,), f32), dma((3,))],
        compiler_params=pltpu.CompilerParams(vmem_limit_bytes=8 * 2**20),
        name="finish",
    )(raw, result)


def solution(mesh):
    in_specs = (P(("loop", "group"), None), P(("loop", "group"), None), P(), P())
    out_specs = (P(("loop", "group"), None), P(("loop", "group"), None), P())
    return jax.shard_map(body, mesh=mesh, in_specs=in_specs, out_specs=out_specs, check_vma=False)
```

```python
import functools

import jax
import jax.numpy as jnp
from jax import lax
from jax.experimental import pallas as pl
from jax.experimental.pallas import tpu as pltpu
from jax.sharding import PartitionSpec as P

STEPS = 2
EPS = 1e-06
MESH = pl.DeviceIdType.MESH

CHUNK = 32
LAST = (256, 128, 128)
LEAD = 3
HELD = 2
LEAD_FIRST = 8
PASS = 256

IMG, TXT, IMG2, TXT2, IMG1, TXT1 = range(6)
N_Y, N_CORE = 4, 2


def project(values, scale, direction):
    unit = values.astype(jnp.float32) * scale
    inner = jnp.sum(unit * direction, axis=1, keepdims=True)
    return ((direction - unit * inner) * scale).astype(jnp.bfloat16)


def kernel(
    n_loop,
    log_temp,
    logit_bias,
    images,
    texts,
    raw,
    result,
    acc,
    inverse,
    land,
    sums,
    tiles_z,
    tiles_p,
    load_sem,
    near_send,
    far_send,
    arrived,
    z_ready,
    relayed,
    group_ready,
    z_send,
    z_recv,
    p_send,
    p_recv,
):
    rows = raw.shape[1]
    chunks = rows // CHUNK
    n_z = n_loop // 2

    loads = [
        pltpu.make_async_copy(source, raw.at[block], load_sem.at[block])
        for block, source in ((IMG, images), (TXT, texts))
    ]
    for load in loads:
        load.start()

    p = lax.axis_index("loop")
    h = lax.axis_index("group")
    z, xh = p // 2, lax.rem(p, 2)
    xl, yc = h // (N_Y * N_CORE), lax.rem(h, N_Y * N_CORE)

    def at(z_, xh_, xl_, yc_):
        return (z_ * 2 + xh_, xl_ * (N_Y * N_CORE) + yc_)

    up = lax.rem(z + 1, n_z)
    down = lax.rem(z + n_z - 1, n_z)
    across = at(z, 1 - xh, xl, yc)
    above = at(up, xh, xl, yc)
    below = at(down, xh, xl, yc)

    def z_peer(i):
        return at(i, xh, xl, yc)

    def plane_peer(i):
        return at(z, i // (2 * N_Y * N_CORE), lax.rem(i // (N_Y * N_CORE), 2), lax.rem(i, N_Y * N_CORE))

    spots = 4 * N_Y * N_CORE
    groups = (
        (tiles_z, z, n_z, n_z - 5, z_peer, z_send, z_recv),
        (tiles_p, (xh * 2 + xl) * (N_Y * N_CORE) + yc, spots, spots - 1, plane_peer, p_send, p_recv),
    )

    def loop(start, stop, body):
        def step(i, carry):
            body(i)
            return carry

        lax.fori_loop(start, stop, step, 0)

    barrier = pltpu.get_barrier_semaphore()

    def greet(device):
        pl.semaphore_signal(barrier, inc=1, device_id=device, device_id_type=MESH)

    last, collector = n_z - 1, n_z - 5
    greet(across)
    greet(below)
    pl.when(z != last)(lambda: greet(above))
    expected = 3 - jnp.where(z == 0, 1, 0)
    _, place, size, hearer, peer, _, _ = groups[1]
    expected = expected + jnp.where(place == hearer, size - 1, 0)
    pl.when(place != hearer)(functools.partial(greet, peer(hearer)))

    expected = expected + jnp.where(z == last, n_z - 6, jnp.where(z == collector, 4, 0))
    near_collector = jnp.logical_and(z >= collector - 4, z < collector)
    pl.when(near_collector)(lambda: greet(z_peer(collector)))
    pl.when(jnp.logical_or(z < collector - 4, jnp.logical_and(z > collector, z < last)))(lambda: greet(z_peer(last)))

    first = 1 - xh

    def part(c):
        return pl.ds(pl.multiple_of(c * CHUNK, CHUNK), CHUNK)

    def normalize(block):
        def step(c):
            here = pl.ds(pl.multiple_of(c * PASS, PASS), PASS)
            values = raw[block, here].astype(jnp.float32)
            length = jnp.sqrt(jnp.sum(values * values, axis=1, keepdims=True) + EPS)
            scale = 1.0 / length
            inverse[block, here] = scale
            land[block, here] = (values * scale).astype(jnp.bfloat16)

        loop(0, rows // PASS, step)

    def own_copy(c):
        return pltpu.make_async_remote_copy(
            src_ref=land.at[first, part(c)],
            dst_ref=land.at[4 + first, part(c)],
            send_sem=far_send.at[0],
            recv_sem=arrived.at[2 + first, c],
            device_id=across,
            device_id_type=MESH,
        )

    def forward_copy(c):
        return pltpu.make_async_remote_copy(
            src_ref=land.at[2 + xh, part(c)],
            dst_ref=land.at[4 + xh, part(c)],
            send_sem=far_send.at[1],
            recv_sem=arrived.at[2 + xh, c],
            device_id=across,
            device_id_type=MESH,
        )

    def near_copy(block, c):
        return pltpu.make_async_remote_copy(
            src_ref=land.at[block, part(c)],
            dst_ref=land.at[2 + block, part(c)],
            send_sem=near_send.at[block],
            recv_sem=arrived.at[block, c],
            device_id=below if block == IMG else above,
            device_id_type=MESH,
        )

    def wait_arrival(slot, c):
        pltpu.make_async_remote_copy(
            src_ref=land.at[slot, part(c)],
            dst_ref=land.at[slot, part(c)],
            send_sem=near_send.at[0],
            recv_sem=arrived.at[slot - 2, c],
            device_id=across,
            device_id_type=MESH,
        ).wait_recv()

    for block in (IMG, TXT):
        loads[block].wait()
        normalize(block)
    pl.semaphore_wait(barrier, expected)

    @pl.when(z == last)
    def _():
        pl.semaphore_signal(z_ready, inc=1, device_id=above, device_id_type=MESH)

    lead = jnp.where(z == 0, LEAD_FIRST, LEAD)
    loop(0, lead, lambda c: own_copy(c).start())

    @pl.when(z == last)
    def _():
        pl.semaphore_signal(relayed.at[0], inc=1, device_id=z_peer(collector + 1), device_id_type=MESH)

    pl.when(z == 0)(functools.partial(pl.semaphore_wait, z_ready, 1))
    loop(0, chunks, lambda c: near_copy(IMG, c).start())
    pl.when(xh == 1)(lambda: loop(lead, chunks, lambda c: own_copy(c).start()))
    loop(0, chunks, lambda c: near_copy(TXT, c).start())

    def tell_group(k):
        _, place, size, collector, peer, _, _ = groups[k]

        def tell(i):
            device = peer(lax.rem(collector + i, size))
            pl.semaphore_signal(group_ready.at[k], inc=1, device_id=device, device_id_type=MESH)

        pl.when(place == collector)(lambda: loop(1, size, tell))

    temper = jnp.exp(log_temp[...].reshape(1, 1))
    offset = logit_bias[...].reshape(1, 1)
    sums[...] = jnp.zeros_like(sums)

    def fold(values):
        total = jnp.sum(values.reshape(rows // 8, 8, values.shape[1]), axis=0)
        return sum(total[:, k : k + 128] for k in range(0, values.shape[1], 128))

    def piece(own, slot, start, size, matched=False, loss=False, after_loss=None):
        partner = land[slot, start : start + size]
        scores = lax.dot_general(
            land[own], partner, (((1,), (1,)), ((), ())), preferred_element_type=jnp.float32
        )
        logit = temper * scores + offset
        if matched:
            r = lax.broadcasted_iota(jnp.int32, (rows, size), 0)
            c = lax.broadcasted_iota(jnp.int32, (rows, size), 1) + start
            logit = jnp.where(r == c, -logit, logit)
        small = jnp.exp(-jnp.abs(logit))
        recip = 1.0 / (1.0 + small)
        slope = jnp.where(logit >= 0, recip, small * recip)
        if matched:
            slope = jnp.where(r == c, -slope, slope)
        if loss:
            sums[0] += fold(jnp.maximum(logit, 0.0) + jnp.log1p(small))
            sums[1] += fold(slope * scores)
            sums[2] += fold(slope)
        if after_loss:
            after_loss()
        weighted = (temper * slope).astype(jnp.bfloat16)
        direction = jnp.dot(weighted, partner, preferred_element_type=jnp.float32)
        if matched:
            acc[own] = direction
        else:
            acc[own] += direction

    def project_block(block, c):
        here = pl.ds(pl.multiple_of(c * PASS, PASS), PASS)
        raw[block, here] = project(raw[block, here], inverse[block, here], acc[block, here])

    def last_piece(start, size):
        partner = land[TXT1, start : start + size]
        for first_row in range(0, rows, PASS):
            here = pl.ds(first_row, PASS)
            scores = lax.dot_general(
                land[IMG, here], partner, (((1,), (1,)), ((), ())), preferred_element_type=jnp.float32
            )
            logit = temper * scores + offset
            small = jnp.exp(-jnp.abs(logit))
            recip = 1.0 / (1.0 + small)
            slope = jnp.where(logit >= 0, recip, small * recip)
            weighted = (temper * slope).astype(jnp.bfloat16)
            direction = acc[IMG, here] + jnp.dot(weighted, partner, preferred_element_type=jnp.float32)
            raw[IMG, here] = project(raw[IMG, here], inverse[IMG, here], direction)

    def hand_on(c):
        wait_arrival(2 + xh, c)
        forward_copy(c).start()

    def piece_of(own, slot, start, size, **kinds):
        if slot in (IMG1, TXT1):
            loop(start // CHUNK, (start + size) // CHUNK, lambda c: wait_arrival(slot, c))
        piece(own, slot, start, size, **kinds)

    def rest(c):
        wait_arrival(3 - xh, c)

    part_rows = rows // 2
    middle = chunks // 2
    loop(0, 2, hand_on)
    piece(TXT, IMG, 0, rows, matched=True, loss=True)
    loop(2, 4, hand_on)

    @pl.when(z == collector + 1)
    def _():
        pl.semaphore_wait(relayed.at[0], 1)
        pl.semaphore_signal(relayed.at[1], inc=1, device_id=z_peer(collector), device_id_type=MESH)

    piece(IMG, TXT, 0, rows, matched=True)
    loop(4, middle, hand_on)
    pl.when(z == collector)(functools.partial(pl.semaphore_wait, relayed.at[1], 1))
    for k in range(len(groups)):
        tell_group(k)
    pl.when(xh == 1)(lambda: loop(0, middle, rest))
    piece(TXT, IMG2, 0, part_rows, loss=True)
    loop(middle, middle + 4, hand_on)
    piece_of(TXT, IMG1, 0, part_rows, loss=True)
    loop(middle + 4, chunks - HELD, hand_on)
    loop(chunks - HELD, chunks, lambda c: wait_arrival(2 + xh, c))

    @pl.when(xh == 0)
    def _():
        loop(chunks - HELD, chunks, lambda c: forward_copy(c).start())
        loop(lead, chunks - HELD, lambda c: own_copy(c).start())

    pl.when(xh == 1)(lambda: loop(middle, chunks, rest))
    piece(TXT, IMG2, part_rows, part_rows, loss=True)
    piece_of(TXT, IMG1, part_rows, part_rows // 2, loss=True)
    def sums_of_device():
        lane = lax.broadcasted_iota(jnp.int32, (1, 128), 1)
        partial = jnp.zeros((1, 128), jnp.float32)
        n_pairs = n_loop * lax.axis_size("group") * rows * rows * (STEPS + 1)
        for k, factor in enumerate((1.0, temper, 1.0)):
            total = jnp.sum(jnp.sum(sums[k], axis=0, keepdims=True), axis=1, keepdims=True) * factor / n_pairs
            partial = jnp.where(lane == k, total, partial)
        return partial

    def exchange_copy(k, source, target, device):
        tiles, _, _, _, _, send, recv = groups[k]
        return pltpu.make_async_remote_copy(
            src_ref=tiles.at[source],
            dst_ref=tiles.at[target],
            send_sem=send,
            recv_sem=recv,
            device_id=device,
            device_id_type=MESH,
        )

    def line_order():
        steps = sorted(range(1, n_z), key=lambda i: -min(i, n_z - i))
        return [z_peer(lax.rem(z + i, n_z)) for i in steps]

    def plane_order():
        x, y, core = xh * 2 + xl, yc // N_CORE, lax.rem(yc, N_CORE)
        columns = [lax.rem(x + i, 4) for i in (2, 1, 3, 0)]
        columns = [(z * 2 + c // 2, lax.rem(c, 2) * (N_Y * N_CORE)) for c in columns]
        spots_y = [lax.rem(y + i, N_Y) * N_CORE for i in (2, 1, 3, 0)]
        spots_of = [s + lax.rem(core + i, N_CORE) for s in spots_y for i in (1, 0)]
        return [(at_loop, at_group + s) for at_loop, at_group in columns for s in spots_of][:-1]

    def exchange_start(k, value):
        tiles, place, _, collector, _, _, _ = groups[k]
        tiles[place] = value
        pl.when(place != collector)(functools.partial(pl.semaphore_wait, group_ready.at[k], 1))
        for device in line_order() if k == 0 else plane_order():
            exchange_copy(k, place, place, device).start()

    def exchange_end(k):
        tiles, _, size, _, _, _, _ = groups[k]
        others = pl.ds(0, size - 1)
        exchange_copy(k, others, others, across).wait_recv()
        return jnp.sum(tiles[...], axis=0)

    def exchange_sent(k):
        others = pl.ds(0, groups[k][2] - 1)
        exchange_copy(k, others, others, across).wait_send()

    piece_of(
        TXT,
        IMG1,
        part_rows + part_rows // 2,
        part_rows // 2,
        loss=True,
        after_loss=lambda: exchange_start(0, sums_of_device()),
    )
    pl.when(xh == 0)(lambda: loop(0, chunks, rest))
    piece(IMG, TXT2, 0, rows)
    loop(0, rows // PASS, functools.partial(project_block, TXT))

    def all_sent(semaphore):
        pltpu.make_async_remote_copy(
            src_ref=land.at[IMG],
            dst_ref=land.at[IMG2],
            send_sem=semaphore,
            recv_sem=arrived.at[0, 0],
            device_id=across,
            device_id_type=MESH,
        ).wait_send()

    start = 0
    for k, size in enumerate(LAST):
        if k == 1:
            exchange_start(1, exchange_end(0))
            pl.when(xh == 0)(lambda: loop(chunks - HELD, chunks, lambda c: own_copy(c).start()))
            pl.when(xh == 1)(lambda: loop(chunks - HELD, chunks, lambda c: forward_copy(c).start()))
        if k == len(LAST) - 1:
            all_sent(near_send.at[IMG])
            all_sent(near_send.at[TXT])
        if k < len(LAST) - 1:
            piece_of(IMG, TXT1, start, size)
            start += size

    loop(start // CHUNK, chunks, lambda c: wait_arrival(TXT1, c))
    last_piece(start, rows - start)
    result[...] = exchange_end(1)
    exchange_sent(0)
    exchange_sent(1)
    all_sent(far_send.at[0])
    all_sent(far_send.at[1])


def finish_kernel(raw, result, image_grad, text_grad, summary, totals, sem):
    copies = [
        pltpu.make_async_copy(raw.at[IMG], image_grad, sem.at[0]),
        pltpu.make_async_copy(raw.at[TXT], text_grad, sem.at[1]),
        pltpu.make_async_copy(totals, summary, sem.at[2]),
    ]
    copies[0].start()
    copies[1].start()
    lane = lax.broadcasted_iota(jnp.int32, (1, 128), 1)
    for k in range(3):
        totals[k] = jnp.sum(jnp.where(lane == k, result[...], 0.0))
    copies[2].start()
    for copy in copies:
        copy.wait()


def body(images, texts, log_temp, logit_bias):
    rows, width = images.shape
    chunks = rows // CHUNK
    n_loop = lax.axis_size("loop")
    n_z, spots = n_loop // 2, 4 * N_Y * N_CORE
    bf16, f32, dma = jnp.bfloat16, jnp.float32, pltpu.SemaphoreType.DMA
    hbm = pl.BlockSpec(memory_space=pltpu.HBM)
    vmem = pl.BlockSpec(memory_space=pltpu.VMEM)
    raw, result = pl.pallas_call(
        functools.partial(kernel, n_loop),
        out_shape=(
            jax.ShapeDtypeStruct((2, rows, width), bf16),
            jax.ShapeDtypeStruct((1, 128), f32),
        ),
        in_specs=[vmem, vmem, hbm, hbm],
        out_specs=(vmem,) * 2,
        scratch_shapes=[
            pltpu.VMEM((2, rows, width), f32),
            pltpu.VMEM((2, rows, 1), f32),
            pltpu.VMEM((6, rows, width), bf16),
            pltpu.VMEM((3, 8, 128), f32),
            pltpu.VMEM((n_z, 1, 128), f32),
            pltpu.VMEM((spots, 1, 128), f32),
            dma((2,)),
            dma((2,)),
            dma((2,)),
            dma((4, chunks)),
            pltpu.SemaphoreType.REGULAR,
            pltpu.SemaphoreType.REGULAR((2,)),
            pltpu.SemaphoreType.REGULAR((2,)),
            dma(()),
            dma(()),
            dma(()),
            dma(()),
        ],
        compiler_params=pltpu.CompilerParams(
            collective_id=0, has_side_effects=True, vmem_limit_bytes=24 * 2**20
        ),
        cost_estimate=pl.CostEstimate(
            flops=24 * rows * rows * width, bytes_accessed=8 * rows * width, transcendentals=2 * 6 * rows * rows
        ),
        name="exchange",
    )(log_temp, logit_bias, *(pltpu.with_memory_space_constraint(a, pltpu.HBM) for a in (images, texts)))
    return pl.pallas_call(
        finish_kernel,
        out_shape=(
            jax.ShapeDtypeStruct((rows, width), bf16),
            jax.ShapeDtypeStruct((rows, width), bf16),
            jax.ShapeDtypeStruct((3,), f32),
        ),
        in_specs=[vmem] * 2,
        out_specs=(hbm,) * 3,
        scratch_shapes=[pltpu.SMEM((3,), f32), dma((3,))],
        compiler_params=pltpu.CompilerParams(vmem_limit_bytes=8 * 2**20),
        name="finish",
    )(raw, result)


def solution(mesh):
    in_specs = (P(("loop", "group"), None), P(("loop", "group"), None), P(), P())
    out_specs = (P(("loop", "group"), None), P(("loop", "group"), None), P())
    return jax.shard_map(body, mesh=mesh, in_specs=in_specs, out_specs=out_specs, check_vma=False)
```
